128 devices in a mesh: slab: 2 (over z_hi), row: 4 (over z_lo, core), col: 16 (over x, y).
Axes of the slice: x: 4, y: 4, z: 4 (z_hi: 2, z_lo: 2; z = z_hi * 2 + z_lo), core: 2. Of those that a mesh axis runs over, the one named last changes fastest.
Arguments:
- distances: bfloat16 [1024, 4096], P(('slab', 'row', 'col')), may hold values from 0.19921875 to 2
- projection: bfloat16 [4096, 4, 2, 2048], P(None, None, None, 'col'), may hold values from -0.25 to 0.25
- phases: float32 [4, 2, 2048], P(None, None, 'col'), may hold values from -3.140625 to 3.140625
- segment_ids: int32 [1024], replicated, may hold values from 0 to 7, never falling along the last dimension, each value on 1 to 192 neighbouring positions
Outputs:
- instant_cov: float32 [16384, 4, 2, 2048], P('row', None, 'slab', 'col')
- lagged_cov: float32 [16384, 4, 2, 2048], P('row', None, 'slab', 'col')
The draws below stay inside these ranges and needn't reach their ends.
Inputs may be any that keep to these rules, and one draw needn't show every extreme that they name: `segment_ids`: segment ids never fall along the frames; each segment holds 1 to 192 frames and one holds exactly 192.
All inputs are finite; a program needn't handle non-finite values.
Results may differ from the reference program's by a relative error of at most 0.0011.
Values may be sent and summed in bfloat16 or wider, within the bound.
A program may use at most 192 MiB of HBM per device.

```python
import math
import jax
import jax.numpy as jnp
import numpy as np
from jax import lax

D_IN = 4096
F = 16384
LAG = 50
SEG_MOST = 192
FRAMES = 1024
SEGMENTS = 8
FPART = 2048
N_SLAB = 2
N_ROW = 4


def block_levels(stream_key, shape, shards, low, high):
    level, own = 1.0, jax.random.fold_in(stream_key, 6)
    for dim, parts in shards:
        draws = jnp.exp(jax.random.uniform(jax.random.fold_in(own, dim), (parts,), jnp.float32, low / len(shards), high / len(shards)))
        level = level * jnp.repeat(draws, shape[dim] // parts).reshape([-1 if axis == dim else 1 for axis in range(len(shape))])
    return level


def profile(amount, total, limit, slope):
    weights = [(1 << 20) // math.isqrt(standing ** slope) + 1 for standing in range(2, amount + 1)]
    surplus, counts = total - limit - (amount - 1), [1] * (amount - 1)
    while surplus > 0:
        movable = [i for i in range(amount - 1) if counts[i] < limit]
        mass, left = sum([weights[i] for i in movable]), surplus
        for i in movable:
            extra = min(limit - counts[i], max(1, left * weights[i] // mass), surplus)
            counts[i] = counts[i] + extra
            surplus = surplus - extra
    return np.array([limit] + counts)


def ragged(rng, number_of, total, reach, slope):
    if number_of == 2:
        one = jax.random.randint(rng, (), max(1, total - reach), min(reach, total - 1) + 1)
        return jnp.stack([one, total - one])
    tallies = jnp.asarray(profile(number_of, total, reach, slope), jnp.int32)
    twos = (number_of - 1) // 2
    giver, sink = tallies[1:1 + 2 * twos:2], tallies[2:2 + 2 * twos:2]
    slack = jnp.minimum(giver - 1, reach - sink)
    moved = jax.random.randint(jax.random.fold_in(rng, 1), (twos,), 0, 1 << 20) % (slack + 1)
    tallies = tallies.at[1:1 + 2 * twos:2].set(giver - moved).at[2:2 + 2 * twos:2].set(sink + moved)
    return tallies[jax.random.permutation(jax.random.fold_in(rng, 2), number_of)]


def gaussian(rng, shape, scale, reach, pieces=(), kind=jnp.bfloat16):
    entries = jax.random.normal(rng, shape, jnp.float32) * scale
    if len(pieces) > 0:
        entries = block_levels(rng, shape, pieces, -0.22, 0.18) * entries
    return jnp.clip(entries, min=-reach, max=reach).astype(kind)


def setup_inputs(seed: int = 0) -> dict:
    keys = jax.random.split(jax.random.key(seed), 5)
    return {
        "distances": jnp.clip(0.19921875 + 1.8007812 * jax.random.uniform(keys[0], (FRAMES, D_IN), jnp.float32) ** block_levels(keys[0], (FRAMES, D_IN), ((0, 128),), -0.2, 0.2), 0.19921875, 2.0).astype(jnp.bfloat16),
        "projection": gaussian(keys[1], (D_IN, N_ROW, N_SLAB, FPART), (D_IN // 8) ** -0.5, 0.25, ((3, 16),)),
        "phases": jnp.clip(jax.random.uniform(keys[2], (N_ROW, N_SLAB, FPART), jnp.float32, -3.140625, 3.140625), -3.140625, 3.140625),
        "segment_ids": jnp.searchsorted(jnp.cumsum(ragged(keys[3], SEGMENTS, FRAMES, SEG_MOST, 2)), jnp.arange(FRAMES), side="right").astype(jnp.int32),
    }


def reference(distances, projection, phases, segment_ids):
    flat_projection = projection.reshape(D_IN, F)
    angles = jnp.dot(distances, flat_projection, preferred_element_type=jnp.float32) + phases.reshape(1, F)
    features = jnp.cos(angles).astype(jnp.bfloat16)
    segment_next = jnp.concatenate([segment_ids[LAG:], jnp.full((LAG,), -1, jnp.int32)], 0)
    paired = (segment_ids == segment_next).astype(jnp.int32)
    pair_count = jnp.sum(paired.astype(jnp.float32))
    shifted = jnp.concatenate([features[LAG:], jnp.zeros((LAG, F), jnp.bfloat16)], 0)
    weighted = features * paired.astype(jnp.bfloat16)[:, None]
    contract = (((0,), (0,)), ((), ()))
    instant = lax.dot_general(features, features, contract, preferred_element_type=jnp.float32)
    lagged = lax.dot_general(weighted, shifted, contract, preferred_element_type=jnp.float32)
    tile_shape = (F, N_ROW, N_SLAB, F // (N_ROW * N_SLAB))
    return (instant / jnp.float32(FRAMES)).reshape(tile_shape), (lagged / pair_count).reshape(tile_shape)
```

```python
import functools

import jax
import jax.numpy as jnp
from jax import lax
from jax.experimental import pallas as pl
from jax.experimental.pallas import tpu as pltpu
from jax.sharding import PartitionSpec as P

LAG = 50
MESH = pl.DeviceIdType.MESH
MIB = 1 << 20
PI_A, PI_B, PI_C = 3.140625, 0.0009670257568359375, 6.2771141529083252e-07
COS_POLY = (
    2.08767570e-09, -2.75573192e-07, 2.48015873e-05, -1.38888889e-03, 4.16666667e-02, -0.5, 1.0
)


def cosine(angle):
    k = jnp.floor(angle * (1.0 / 3.14159265358979) + 0.5)
    r = ((angle - k * PI_A) - k * PI_B) - k * PI_C
    odd = k - 2.0 * jnp.floor(k * 0.5)
    square = r * r
    value = jnp.full_like(square, COS_POLY[0])
    for term in COS_POLY[1:]:
        value = value * square + term
    return value * (1.0 - 2.0 * odd)


def positions():
    slab, row, col = lax.axis_index("slab"), lax.axis_index("row"), lax.axis_index("col")
    return col // 4, col % 4, slab * 2 + row // 2, row % 2


def device(x, y, z, k):
    x, y, z, k = x % 4, y % 4, z % 4, k % 2
    return (z // 2, (z % 2) * 2 + k, x * 4 + y)


def remote(src, dst, send, recv, target):
    return pltpu.make_async_remote_copy(
        src_ref=src, dst_ref=dst, send_sem=send, recv_sem=recv, device_id=target, device_id_type=MESH
    )


def gather_kernel(
    d_ref, p_ref, phase_ref, left_ref, right_ref,
    stage, planes, d_all, d_rows, natural, turned,
    p_sem, d_send, d_recv, l_send, l_recv, r_send, r_recv, g_send, g_recv, own_sem,
):
    x, y, z, k = positions()
    me = z * 2 + k
    n_chunk = 8
    chunk = p_ref.shape[0] // n_chunk

    def p_copy(n):
        rows = pl.ds(n * chunk, chunk)
        return pltpu.make_async_copy(p_ref.at[rows], stage.at[rows], p_sem.at[n])

    for n in range(n_chunk):
        p_copy(n).start()

    for h in range(2):
        low = d_ref[:, h * 1024:(h + 1) * 1024].astype(jnp.float32)
        high = d_ref[:, 2048 + h * 1024:2048 + (h + 1) * 1024].astype(jnp.float32)
        d_all[h, x, y] = jnp.concatenate([low, high], 0).astype(jnp.bfloat16)

    hops = (1, 3, 2)
    along_x = [device(x + d, y, z, k) for d in hops]
    along_y = [device(x, y + d, z, k) for d in hops]
    mates = [(0, 1), (1, 0), (1, 1), (3, 0), (3, 1), (2, 0), (2, 1)]
    barrier = pltpu.get_barrier_semaphore()
    partners = along_x + along_y + [device(x, y, z + dz, k + dk) for dz, dk in mates]
    for partner in partners:
        pl.semaphore_signal(barrier, inc=1, device_id=partner, device_id_type=MESH)
    pl.semaphore_wait(barrier, len(partners))

    first = []
    for i in range(3):
        own = d_all.at[0, x, y]
        first.append(remote(own, own, d_send.at[0, i], d_recv.at[0, i], along_x[i]))
        own = d_all.at[1, x, y]
        first.append(remote(own, own, d_send.at[1, i], d_recv.at[1, i], along_y[i]))
    for copy in first:
        copy.start()

    to = lax.broadcasted_iota(jnp.int32, (256, 256), 0)
    source = lax.broadcasted_iota(jnp.int32, (256, 256), 1)
    permute = jnp.where((to % 32) * 8 + to // 32 == source, 1.0, 0.0).astype(jnp.bfloat16)

    def sort_rows(n, _):
        rows = stage[pl.ds(pl.multiple_of(n * 1024, 1024), 1024), :]
        wide = jnp.concatenate([rows[q * 256:(q + 1) * 256] for q in range(4)], 1)
        out = jnp.dot(permute, wide, preferred_element_type=jnp.float32).astype(jnp.bfloat16)
        for a in range(4):
            for b in range(2):
                part = out[(a * 2 + b) * 32:(a * 2 + b + 1) * 32]
                for q in range(4):
                    at = pl.ds(pl.multiple_of(n * 128 + q * 32, 32), 32)
                    planes[a, at, b * 128:(b + 1) * 128] = part[:, q * 128:(q + 1) * 128]
        return 0

    for n in range(3):
        p_copy(n).wait()
    lax.fori_loop(0, 12, sort_rows, 0)

    for copy in first:
        copy.wait_recv()
    second = []
    for i in range(3):
        line = d_all.at[0, :, y]
        second.append(remote(line, line, d_send.at[0, 3 + i], d_recv.at[0, 3 + i], along_y[i]))
        line = d_all.at[1, x]
        second.append(remote(line, line, d_send.at[1, 3 + i], d_recv.at[1, 3 + i], along_x[i]))
    for copy in second:
        copy.start()
    for n in range(3, n_chunk):
        p_copy(n).wait()
    lax.fori_loop(12, 32, sort_rows, 0)
    for copy in second:
        copy.wait_recv()

    for h in range(2):
        for q in range(2):
            part = d_all[h].astype(jnp.float32).reshape(16, 16, 1024)[:, q * 8:(q + 1) * 8, :]
            at = q * 2048 + h * 1024
            d_rows[:, at:at + 1024] = part.reshape(128, 1024).astype(jnp.bfloat16)

    def features(step, _):
        a = (z % 2 * 2 + k + step) % 4
        angles = jnp.dot(d_rows[...], planes[a], preferred_element_type=jnp.float32)
        shift = phase_ref[pl.ds(a, 1)].reshape(2, 128)
        for b in range(2):
            value = cosine(angles[:, b * 128:(b + 1) * 128] + shift[b:b + 1])
            natural[b, a] = value.astype(jnp.bfloat16)
            turned[a, b] = value.T.astype(jnp.bfloat16)
        return 0

    lax.fori_loop(0, 4, features, 0)

    own_left = pltpu.make_async_copy(turned.at[z % 2 * 2 + k], left_ref.at[me, :, x, y], own_sem.at[0])
    own_right = pltpu.make_async_copy(natural.at[z // 2], right_ref.at[me], own_sem.at[1])
    own_left.start()
    own_right.start()
    lefts, rights = [], []
    for i, (dz, dk) in enumerate(mates):
        z2, k2 = (z + dz) % 4, (k + dk) % 2
        target = device(x, y, z2, k2)
        j = mates.index((-dz % 4, dk))
        lefts.append(remote(
            turned.at[z2 % 2 * 2 + k2], left_ref.at[me, :, x, y], l_send.at[i], l_recv.at[j], target))
        rights.append(remote(natural.at[z2 // 2], right_ref.at[me], r_send.at[i], r_recv.at[j], target))
    for copy in lefts + rights:
        copy.start()
    own_left.wait()

    def slot(step):
        e = step // 2
        dz = e + e // 2 - 2 * (e // 3)
        return (z + dz) % 4 * 2 + (k + step) % 2

    px, mx, py, my = along_x[0], along_x[1], along_y[0], along_y[1]
    xp, xm, yp, ym = (x + 1) % 4, (x + 3) % 4, (y + 1) % 4, (y + 3) % 4

    def copies(group, number):
        g = slot(group)
        half0, half1 = left_ref.at[g, 0], left_ref.at[g, 1]
        low, high = pl.ds(0, 64), pl.ds(64, 64)
        if number == 0:
            pairs = [(half0.at[x, y], px), (half0.at[x, y], mx), (half1.at[x, y], py), (half1.at[x, y], my)]
        elif number == 1:
            pairs = [(half0.at[xm, y, low], px), (half0.at[xp, y, high], mx),
                     (half1.at[x, ym, low], py), (half1.at[x, yp, high], my)]
        elif number == 2:
            pairs = [(half0.at[:, y], py), (half0.at[:, y], my), (half1.at[x], px), (half1.at[x], mx)]
        else:
            pairs = [(half0.at[pl.ds(0, 2), ym], py), (half0.at[pl.ds(2, 2), yp], my),
                     (half1.at[xm, pl.ds(0, 2)], px), (half1.at[xp, pl.ds(2, 2)], mx)]
        return [
            remote(ref, ref, g_send.at[group, number, i], g_recv.at[group, number, i], target)
            for i, (ref, target) in enumerate(pairs)
        ]

    def rounds(step, _):
        for number in range(5):
            group = step - number

            @pl.when(jnp.logical_and(group >= 0, group < 8))
            def _():
                if number > 0:
                    for copy in copies(group, number - 1):
                        copy.wait_recv()
                if number < 4:
                    if number == 0:
                        @pl.when(group > 0)
                        def _():
                            at = left_ref.at[me, :, x, y]
                            i = group - 1
                            remote(at, at, l_send.at[i], l_recv.at[i], px).wait_recv()
                    for copy in copies(group, number):
                        copy.start()
        return 0

    lax.fori_loop(0, 12, rounds, 0)

    own_right.wait()
    for copy in rights:
        copy.wait()
    for copy in lefts + first + second:
        copy.wait_send()

    def drain(group, _):
        for number in range(4):
            for copy in copies(group, number):
                copy.wait_send()
        return 0

    lax.fori_loop(0, 8, drain, 0)


def gather(distances, projection, phases):
    bf16 = jnp.bfloat16
    dma = pltpu.SemaphoreType.DMA
    return pl.pallas_call(
        gather_kernel,
        out_shape=(
            pltpu.VMEM((8, 2, 4, 4, 128, 128), bf16),
            pltpu.VMEM((8, 4, 128, 128), bf16),
        ),
        in_specs=[
            pl.BlockSpec(memory_space=pltpu.VMEM),
            pl.BlockSpec(memory_space=pl.ANY),
            pl.BlockSpec(memory_space=pltpu.VMEM),
        ],
        out_specs=(pl.BlockSpec(memory_space=pltpu.VMEM), pl.BlockSpec(memory_space=pltpu.VMEM)),
        scratch_shapes=[
            pltpu.VMEM((32768, 128), bf16),
            pltpu.VMEM((4, 4096, 256), bf16),
            pltpu.VMEM((2, 4, 4, 16, 1024), bf16),
            pltpu.VMEM((128, 4096), bf16),
            pltpu.VMEM((2, 4, 128, 128), bf16),
            pltpu.VMEM((4, 2, 128, 128), bf16),
            dma((8,)),
            dma((2, 6)),
            dma((2, 6)),
            dma((7,)),
            dma((7,)),
            dma((7,)),
            dma((7,)),
            dma((8, 4, 4)),
            dma((8, 4, 4)),
            dma((2,)),
        ],
        compiler_params=pltpu.CompilerParams(
            collective_id=0, has_side_effects=True, vmem_limit_bytes=44 * MIB
        ),
        name="gather_features",
    )(distances, projection, phases)


def covariance_kernel(left_ref, right_ref, segment_ref, instant_ref, lagged_ref, columns, scale):
    bf16, f32 = jnp.bfloat16, jnp.float32

    @pl.when(pl.program_id(0) == 0)
    def _():
        for g in range(8):
            for a in range(4):
                columns[g * 128:(g + 1) * 128, a * 128:(a + 1) * 128] = right_ref[g, a]
        ids = jnp.broadcast_to(segment_ref[...], (8, 1024))
        frame = lax.broadcasted_iota(jnp.int32, (8, 1024), 1)
        paired = jnp.where((pltpu.roll(ids, LAG, 1) == ids) & (frame >= LAG), 1.0, 0.0).astype(f32)
        scale[0] = 1.0 / jnp.sum(paired[0:1])
        for n in range(8):
            start = min(n * 128, 768)
            here = lax.broadcasted_iota(jnp.int32, (128, 256), 0) + n * 128
            there = lax.broadcasted_iota(jnp.int32, (128, 256), 1) + start
            take = jnp.where(there == here + LAG, paired[0:1, start:start + 256], 0.0).astype(bf16)
            moved = jnp.dot(take, columns[start:start + 256, 0:512], preferred_element_type=f32)
            columns[n * 128:(n + 1) * 128, 512:1024] = moved.astype(bf16)

    rows = jnp.concatenate(
        [jnp.concatenate([left_ref[g, 0, 0, i] for g in range(8)], 1) for i in range(4)], 0
    )
    inverse = scale[0]
    for out_ref, at, factor in ((instant_ref, 0, 1.0 / 1024), (lagged_ref, 512, inverse)):
        total = jnp.dot(rows, columns[:, at:at + 512], preferred_element_type=f32) * factor
        for a in range(4):
            out_ref[pl.ds(a, 512, stride=4), :] = total[:, a * 128:(a + 1) * 128]


def covariances(left, right, segment_ids):
    out = jax.ShapeDtypeStruct((16384, 128), jnp.float32)
    return pl.pallas_call(
        covariance_kernel,
        grid=(8,),
        out_shape=(out, out),
        in_specs=[
            pl.BlockSpec((8, 1, 1, 4, 128, 128), lambda m: (0, m // 4, m % 4, 0, 0, 0)),
            pl.BlockSpec((8, 4, 128, 128), lambda m: (0, 0, 0, 0)),
            pl.BlockSpec((1, 1024), lambda m: (0, 0)),
        ],
        out_specs=(pl.BlockSpec((2048, 128), lambda m: (m, 0)), pl.BlockSpec((2048, 128), lambda m: (m, 0))),
        scratch_shapes=[pltpu.VMEM((1024, 1024), jnp.bfloat16), pltpu.SMEM((1,), jnp.float32)],
        compiler_params=pltpu.CompilerParams(vmem_limit_bytes=40 * MIB),
        name="covariances",
    )(left, right, segment_ids)


def per_device(distances, projection, phases, segment_ids):
    left, right = gather(distances, projection.reshape(32768, 128), phases)
    instant, lagged = covariances(left, right, segment_ids.reshape(1, 1024))
    return instant.reshape(4096, 4, 1, 128), lagged.reshape(4096, 4, 1, 128)


def solution(mesh):
    placed = (
        P(("slab", "row", "col"), None),
        P(None, None, None, "col"),
        P(None, None, "col"),
        P(),
    )
    return jax.shard_map(
        per_device,
        mesh=mesh,
        in_specs=placed,
        out_specs=(P("row", None, "slab", "col"), P("row", None, "slab", "col")),
        check_vma=False,
    )
```

```python
import functools

import jax
import jax.numpy as jnp
from jax import lax
from jax.experimental import pallas as pl
from jax.experimental.pallas import tpu as pltpu
from jax.sharding import PartitionSpec as P

LAG = 50
MESH = pl.DeviceIdType.MESH
MIB = 1 << 20
PI_A, PI_B, PI_C = 3.140625, 0.0009670257568359375, 6.2771141529083252e-07
COS_POLY = (
    2.08767570e-09, -2.75573192e-07, 2.48015873e-05, -1.38888889e-03, 4.16666667e-02, -0.5, 1.0
)


def cosine(angle):
    k = jnp.floor(angle * (1.0 / 3.14159265358979) + 0.5)
    r = ((angle - k * PI_A) - k * PI_B) - k * PI_C
    odd = k - 2.0 * jnp.floor(k * 0.5)
    square = r * r
    value = jnp.full_like(square, COS_POLY[0])
    for term in COS_POLY[1:]:
        value = value * square + term
    return value * (1.0 - 2.0 * odd)


def positions():
    slab, row, col = lax.axis_index("slab"), lax.axis_index("row"), lax.axis_index("col")
    return col // 4, col % 4, slab * 2 + row // 2, row % 2


def device(x, y, z, k):
    x, y, z, k = x % 4, y % 4, z % 4, k % 2
    return (z // 2, (z % 2) * 2 + k, x * 4 + y)


def remote(src, dst, send, recv, target):
    return pltpu.make_async_remote_copy(
        src_ref=src, dst_ref=dst, send_sem=send, recv_sem=recv, device_id=target, device_id_type=MESH
    )


def gather_kernel(
    d_hbm, p_ref, phase_hbm, segment_hbm, instant_ref, lagged_ref, left_ref, columns,
    d_ref, phase_ref, segment_ref, stage, planes, d_all, d_rows, partial, natural, turned, right_ref, scale,
    in_sem, p_sem, d_send, d_recv, e_send, e_recv, r_send, r_recv, g_send, g_recv, x_send, x_recv, own_sem,
):
    x, y, z, k = positions()
    me, slab, row = z * 2 + k, z // 2, z % 2 * 2 + k
    n_chunk = 8
    chunk = p_ref.shape[0] // n_chunk

    def p_copy(n):
        rows = pl.ds(n * chunk, chunk)
        return pltpu.make_async_copy(p_ref.at[rows], stage.at[rows], p_sem.at[n])

    d_copy = pltpu.make_async_copy(d_hbm, d_ref, in_sem.at[0])
    phase_copy = pltpu.make_async_copy(phase_hbm, phase_ref, in_sem.at[1])
    segment_copy = pltpu.make_async_copy(segment_hbm, segment_ref, in_sem.at[2])
    d_copy.start()
    phase_copy.start()
    segment_copy.start()
    for n in range(n_chunk):
        p_copy(n).start()

    hops = (1, 3, 2)
    along_x = [device(x + d, y, z, k) for d in hops]
    along_y = [device(x, y + d, z, k) for d in hops]
    mates = [(0, 1), (1, 0), (1, 1), (3, 0), (3, 1), (2, 0), (2, 1)]
    barrier = pltpu.get_barrier_semaphore()
    partners = along_x + along_y + [device(x, y, z + dz, k + dk) for dz, dk in mates]
    for partner in partners:
        pl.semaphore_signal(barrier, inc=1, device_id=partner, device_id_type=MESH)

    d_copy.wait()
    for h in range(2):
        for e in range(2):
            at = h * 1024 + e * 512
            low = d_ref[:, at:at + 512].astype(jnp.float32)
            high = d_ref[:, 2048 + at:2048 + at + 512].astype(jnp.float32)
            d_all[h, e, x, y] = jnp.concatenate([low, high], 0).astype(jnp.bfloat16)
    pl.semaphore_wait(barrier, len(partners))

    first = []
    for i in range(3):
        own = d_all.at[0, :, x, y]
        first.append(remote(own, own, d_send.at[0, i], d_recv.at[0, i], along_x[i]))
        own = d_all.at[1, :, x, y]
        first.append(remote(own, own, d_send.at[1, i], d_recv.at[1, i], along_y[i]))
    for copy in first:
        copy.start()

    to = lax.broadcasted_iota(jnp.int32, (256, 256), 0)
    source = lax.broadcasted_iota(jnp.int32, (256, 256), 1)
    permute = jnp.where((to % 32) * 8 + to // 32 == source, 1.0, 0.0).astype(jnp.bfloat16)

    def sort_rows(n, _):
        part = n // 4
        place = part % 2 * 2048 + part // 2 * 512 + n % 4 * 128
        rows = stage[pl.ds(pl.multiple_of(n * 1024, 1024), 1024), :]
        wide = jnp.concatenate([rows[q * 256:(q + 1) * 256] for q in range(4)], 1)
        out = jnp.dot(permute, wide, preferred_element_type=jnp.float32).astype(jnp.bfloat16)
        for a in range(4):
            for b in range(2):
                part = out[(a * 2 + b) * 32:(a * 2 + b + 1) * 32]
                lanes = slice(a % 2 * 128, a % 2 * 128 + 128)
                for q in range(4):
                    at = pl.ds(pl.multiple_of(place + q * 32, 32), 32)
                    planes[b * 2 + a // 2, at, lanes] = part[:, q * 128:(q + 1) * 128]
        return 0

    for n in range(3):
        p_copy(n).wait()
    lax.fori_loop(0, 12, sort_rows, 0, unroll=4)

    for copy in first:
        copy.wait_recv()
    second = []
    for e in range(2):
        for i in range(3):
            n = 3 + e * 3 + i
            line = d_all.at[0, e, :, y]
            second.append(remote(line, line, d_send.at[0, n], d_recv.at[0, n], along_y[i]))
            line = d_all.at[1, e, x]
            second.append(remote(line, line, d_send.at[1, n], d_recv.at[1, n], along_x[i]))
    for copy in second:
        copy.start()
    for n in range(3, n_chunk):
        p_copy(n).wait()
    lax.fori_loop(12, 32, sort_rows, 0, unroll=4)
    phase_copy.wait()
    segment_copy.wait()

    def arrive(e):
        for copy in second[e * 6:(e + 1) * 6]:
            copy.wait_recv()
        for q in range(2):
            for h in range(2):
                part = d_all[h, e].astype(jnp.float32).reshape(16, 16, 512)[:, q * 8:(q + 1) * 8, :]
                at = e * 2048 + (q * 2 + h) * 512
                d_rows[:, at:at + 512] = part.reshape(128, 512).astype(jnp.bfloat16)

    def product(p, e):
        depth = slice(e * 2048, (e + 1) * 2048)
        return jnp.dot(d_rows[:, depth], planes[p, depth, :], preferred_element_type=jnp.float32)

    arrive(0)
    for p in range(4):
        partial[p] = product(p, 0)
    arrive(1)

    def features(b):
        for p in range(2):
            angles = partial[b * 2 + p] + product(b * 2 + p, 1)
            for i in range(2):
                a = p * 2 + i
                value = cosine(angles[:, i * 128:(i + 1) * 128] + phase_ref[a, b:b + 1])
                natural[b, a] = value.astype(jnp.bfloat16)
                turned[a, b * 4:(b + 1) * 4] = value.T.astype(jnp.bfloat16).reshape(4, 2, 16, 128)

    def frames(ref):
        return ref.at[:, :, x, y, slab, :, pl.ds(pl.multiple_of(row * 128, 128), 128)]

    batches = [(pl.ds(0, 1), None), (pl.ds(1, 2), pl.ds(2, 2)), (pl.ds(3, 4), pl.ds(4, 4))]
    own, shares = [], []
    for n, (slots, chunks) in enumerate(batches):
        mine = pl.ds(slab, 1) if chunks is None else chunks
        own.append(pltpu.make_async_copy(turned.at[row, mine], frames(left_ref.at[slots]), own_sem.at[n]))
        for i, (dz, dk) in enumerate(mates):
            j = mates.index((-dz % 4, dk))
            z2, k2 = (z + dz) % 4, (k + dk) % 2
            theirs = pl.ds(z2 // 2, 1) if chunks is None else chunks
            shares.append(remote(
                turned.at[z2 % 2 * 2 + k2, theirs], frames(left_ref.at[slots]),
                e_send.at[n, i], e_recv.at[n, j], device(x, y, z2, k2)))
    own.append(pltpu.make_async_copy(natural.at[slab], right_ref.at[me], own_sem.at[3]))
    mate = device(x, y, z, k + 1)
    rights = []
    for i, dz in enumerate(hops):
        target = device(x, y, z + dz, k)
        rights.append(remote(
            natural.at[(z + dz) % 4 // 2], right_ref.at[me], r_send.at[i], r_recv.at[hops.index(-dz % 4)], target))
    rights.append(remote(natural.at[slab], right_ref.at[me], r_send.at[3], r_recv.at[3], mate))
    handed = []
    for i, dz in enumerate(hops):
        at = right_ref.at[(z + dz) % 4 * 2 + k]
        handed.append(remote(at, at, r_send.at[4 + i], r_recv.at[4 + i], mate))

    features(0)
    for copy in own[:2] + shares[:14]:
        copy.start()
    features(1)
    for copy in own[2:] + shares[14:] + rights:
        copy.start()
    for copy in own[:3]:
        copy.wait()

    px, mx, py, my = along_x[0], along_x[1], along_y[0], along_y[1]
    xp, xm, yp, ym = (x + 1) % 4, (x + 3) % 4, (y + 1) % 4, (y + 3) % 4

    def copies(slot, number):
        half0, half1 = left_ref.at[slot, 0], left_ref.at[slot, 1]
        if number == 0:
            pairs = [(half0.at[x, y], px), (half0.at[x, y], mx), (half1.at[x, y], py), (half1.at[x, y], my)]
        elif number == 1:
            pairs = [(half0.at[xm, y, 0], px), (half0.at[xp, y, 1], mx),
                     (half1.at[x, ym, 0], py), (half1.at[x, yp, 1], my)]
        elif number == 2:
            pairs = [(half0.at[:, y], py), (half0.at[:, y], my), (half1.at[x], px), (half1.at[x], mx)]
        else:
            pairs = [(half0.at[pl.ds(0, 2), ym], py), (half0.at[pl.ds(2, 2), yp], my),
                     (half1.at[xm, pl.ds(0, 2)], px), (half1.at[xp, pl.ds(2, 2)], mx)]
        return [
            remote(ref, ref, g_send.at[slot, number, i], g_recv.at[slot, number, i], target)
            for i, (ref, target) in enumerate(pairs)
        ]

    def crossing(h):
        return remote(left_ref.at[0, h], left_ref.at[7, h], x_send.at[h], x_recv.at[h], device(x, y, z + 2, k))

    def wait_shares(n):
        for copy in shares[n * 7:(n + 1) * 7]:
            copy.wait_recv()

    def multiply(slot, number):
        b, quarter = number // 4, number % 4
        rows = chunk_rows(left_ref, slot)
        for out_ref, at, factor in ((instant_ref, 0, 1.0 / 1024), (lagged_ref, 512, scale[0])):
            total = jnp.dot(rows, columns[:, at:at + 512], preferred_element_type=jnp.float32) * factor
            for c in range(16):
                for a in range(4):
                    part = total[c * 32:(c + 1) * 32, a * 128:(a + 1) * 128]
                    out_ref[b, c, quarter, pl.ds(a, 32, stride=4), :] = part

    def rounds(step, _):
        for number, lead in ((2, 3), (3, 4), (1, 1), (0, 0), (4, 5)):
            slot = step - lead

            @pl.when(jnp.logical_and(slot >= 0, slot < 7))
            def _():
                if number > 0:
                    for copy in copies(slot, number - 1):
                        copy.wait_recv()
                if number == 0:
                    for n, at in enumerate((0, 1, 3)):
                        pl.when(slot == at)(functools.partial(wait_shares, n))
                if number < 4:
                    for copy in copies(slot, number):
                        copy.start()
                else:
                    @pl.when(slot == 0)
                    def _():
                        for h in range(2):
                            crossing(h).start()

                    for earlier in range(4):
                        for copy in copies(slot, earlier):
                            copy.wait_send()
        return 0

    def job(n, _):
        slot = n + jnp.where(n == 5, 2, 0) - jnp.where(n == 6, 1, 0)

        @pl.when(n == 5)
        def _():
            for h in range(2):
                crossing(h).wait_recv()

        multiply(slot, jnp.where(slot == 7, 1 - slab, jnp.where(slot == 0, slab, slot + 1)))
        return 0

    def later(step, _):
        rounds(step, 0)
        begin = jnp.minimum(2 * (step - 7), 5)
        end = jnp.where(step == 10, 7, jnp.minimum(2 * (step - 6), 5))
        lax.fori_loop(begin, end, job, 0)
        return 0

    lax.fori_loop(0, 6, rounds, 0)
    for copy in rights[:3]:
        copy.wait_recv()
    for copy in handed:
        copy.start()
    lax.fori_loop(6, 7, rounds, 0)
    own[3].wait()
    rights[3].wait_recv()
    for copy in handed:
        copy.wait_recv()
    right_columns(right_ref, segment_ref, columns, scale)
    for copy in first + second + shares + rights + handed:
        copy.wait_send()
    lax.fori_loop(7, 11, later, 0)
    for h in range(2):
        crossing(h).wait_send()
    lax.fori_loop(11, 12, rounds, 0)


def chunk_rows(left_ref, slot):
    return jnp.concatenate(
        [
            jnp.concatenate([left_ref[slot, h, x, y, f] for f in range(2)], 1)
            for x in range(4) for y in range(4) for h in range(2)
        ],
        0,
    )


def paired_before(segment_ref):
    ids = jnp.broadcast_to(segment_ref[...], (8, 1024))
    frame = lax.broadcasted_iota(jnp.int32, (8, 1024), 1)
    return jnp.where((pltpu.roll(ids, LAG, 1) == ids) & (frame >= LAG), 1.0, 0.0)[0:1]


def right_columns(right_ref, segment_ref, columns, scale):
    paired = paired_before(segment_ref)
    scale[0] = 1.0 / jnp.sum(paired)
    for g in range(8):
        for a in range(4):
            columns[g * 128:(g + 1) * 128, a * 128:(a + 1) * 128] = right_ref[g, a]
    for n in range(8):
        start = min(n * 128, 768)
        here = lax.broadcasted_iota(jnp.int32, (128, 256), 0) + n * 128
        there = lax.broadcasted_iota(jnp.int32, (128, 256), 1) + start
        take = jnp.where(there == here + LAG, paired[:, start:start + 256], 0.0).astype(jnp.bfloat16)
        moved = jnp.dot(take, columns[start:start + 256, 0:512], preferred_element_type=jnp.float32)
        columns[n * 128:(n + 1) * 128, 512:1024] = moved.astype(jnp.bfloat16)


TILES = (2, 16, 4, 128, 128)


def gather(distances, projection, phases, segment_ids):
    bf16, f32 = jnp.bfloat16, jnp.float32
    dma = pltpu.SemaphoreType.DMA
    anywhere = pl.BlockSpec(memory_space=pl.ANY)
    vmem = pl.BlockSpec(memory_space=pltpu.VMEM)
    return pl.pallas_call(
        gather_kernel,
        out_shape=(
            pltpu.VMEM(TILES, f32),
            pltpu.VMEM(TILES, f32),
            pltpu.VMEM((8, 2, 4, 4, 2, 16, 512), bf16),
            pltpu.VMEM((1024, 1024), bf16),
        ),
        in_specs=[anywhere] * 4,
        out_specs=(vmem,) * 4,
        scratch_shapes=[
            pltpu.VMEM((8, 4096), bf16),
            pltpu.VMEM((4, 2, 128), f32),
            pltpu.VMEM((1, 1024), jnp.int32),
            pltpu.VMEM((32768, 128), bf16),
            pltpu.VMEM((4, 4096, 256), bf16),
            pltpu.VMEM((2, 2, 4, 4, 16, 512), bf16),
            pltpu.VMEM((128, 4096), bf16),
            pltpu.VMEM((4, 128, 256), f32),
            pltpu.VMEM((2, 4, 128, 128), bf16),
            pltpu.VMEM((4, 8, 2, 16, 128), bf16),
            pltpu.VMEM((8, 4, 128, 128), bf16),
            pltpu.SMEM((1,), f32),
            dma((3,)),
            dma((8,)),
            dma((2, 9)),
            dma((2, 9)),
            dma((3, 7)),
            dma((3, 7)),
            dma((7,)),
            dma((7,)),
            dma((7, 4, 4)),
            dma((7, 4, 4)),
            dma((2,)),
            dma((2,)),
            dma((4,)),
        ],
        compiler_params=pltpu.CompilerParams(
            collective_id=0, has_side_effects=True, vmem_limit_bytes=36 * MIB
        ),
        name="gather_features",
    )(distances, projection, phases, segment_ids)


LAST_SLOT, LAST_CHUNK = 6, 7


def finish_kernel(
    instant_tiles, lagged_tiles, left_ref, columns, segment_ref, instant_ref, lagged_ref, instant_last, lagged_last, sem
):
    copies = []

    def move(source, target, n):
        copy = pltpu.make_async_copy(source, target, sem.at[n])
        copy.start()
        copies.append(copy)

    outs = ((instant_tiles, instant_ref, instant_last), (lagged_tiles, lagged_ref, lagged_last))
    for i, (tiles, out_ref, _) in enumerate(outs):
        move(tiles.at[0], out_ref.at[0], i * 3)
        move(tiles.at[1, :, pl.ds(0, 3)], out_ref.at[1, :, pl.ds(0, 3)], i * 3 + 1)
    rows = chunk_rows(left_ref, LAST_SLOT)
    inverse = 1.0 / jnp.sum(paired_before(segment_ref))
    for i, (_, out_ref, last) in enumerate(outs):
        total = jnp.dot(rows, columns[:, i * 512:(i + 1) * 512], preferred_element_type=jnp.float32)
        total = total * (inverse if i else 1.0 / 1024)
        for c in range(16):
            for a in range(4):
                last[c, pl.ds(a, 32, stride=4), :] = total[c * 32:(c + 1) * 32, a * 128:(a + 1) * 128]
        move(last, out_ref.at[1, :, 3], i * 3 + 2)
    for copy in copies:
        copy.wait()


def finish(tiles, segment_ids):
    out = jax.ShapeDtypeStruct(TILES, jnp.float32)
    vmem = pl.BlockSpec(memory_space=pltpu.VMEM)
    anywhere = pl.BlockSpec(memory_space=pl.ANY)
    return pl.pallas_call(
        finish_kernel,
        out_shape=(out, out),
        in_specs=[vmem] * 5,
        out_specs=(anywhere, anywhere),
        scratch_shapes=[
            pltpu.VMEM((16, 128, 128), jnp.float32),
            pltpu.VMEM((16, 128, 128), jnp.float32),
            pltpu.SemaphoreType.DMA((6,)),
        ],
        compiler_params=pltpu.CompilerParams(vmem_limit_bytes=4 * MIB),
        name="covariances",
    )(*tiles, segment_ids)


def per_device(distances, projection, phases, segment_ids):
    segments = segment_ids.reshape(1, 1024)
    tiles = gather(distances, projection.reshape(32768, 128), phases, segments)
    tiles = [pltpu.with_memory_space_constraint(part, pltpu.VMEM) for part in tiles]
    instant, lagged = finish(tiles, segments)
    return instant.reshape(4096, 4, 1, 128), lagged.reshape(4096, 4, 1, 128)


def solution(mesh):
    placed = (
        P(("slab", "row", "col"), None),
        P(None, None, None, "col"),
        P(None, None, "col"),
        P(),
    )
    return jax.shard_map(
        per_device,
        mesh=mesh,
        in_specs=placed,
        out_specs=(P("row", None, "slab", "col"), P("row", None, "slab", "col")),
        check_vma=False,
    )
```

```python
import functools

import jax
import jax.numpy as jnp
from jax import lax
from jax.experimental import pallas as pl
from jax.experimental.pallas import tpu as pltpu
from jax.sharding import PartitionSpec as P

LAG = 50
MESH = pl.DeviceIdType.MESH
MIB = 1 << 20
PI_A, PI_B, PI_C = 3.140625, 0.0009670257568359375, 6.2771141529083252e-07
COS_POLY = (
    2.08767570e-09, -2.75573192e-07, 2.48015873e-05, -1.38888889e-03, 4.16666667e-02, -0.5, 1.0
)


def cosine(angle):
    k = jnp.floor(angle * (1.0 / 3.14159265358979) + 0.5)
    r = ((angle - k * PI_A) - k * PI_B) - k * PI_C
    odd = k - 2.0 * jnp.floor(k * 0.5)
    square = r * r
    value = jnp.full_like(square, COS_POLY[0])
    for term in COS_POLY[1:]:
        value = value * square + term
    return value * (1.0 - 2.0 * odd)


def positions():
    slab, row, col = lax.axis_index("slab"), lax.axis_index("row"), lax.axis_index("col")
    return col // 4, col % 4, slab * 2 + row // 2, row % 2


def device(x, y, z, k):
    x, y, z, k = x % 4, y % 4, z % 4, k % 2
    return (z // 2, (z % 2) * 2 + k, x * 4 + y)


def remote(src, dst, send, recv, target):
    return pltpu.make_async_remote_copy(
        src_ref=src, dst_ref=dst, send_sem=send, recv_sem=recv, device_id=target, device_id_type=MESH
    )


def gather_kernel(
    d_hbm, p_ref, phase_hbm, segment_hbm, instant_ref, lagged_ref, left_ref, columns,
    d_ref, phase_ref, segment_ref, stage, planes, d_all, d_rows, natural, turned, right_ref, scale,
    in_sem, p_sem, d_send, d_recv, e_send, e_recv, r_send, r_recv, g_send, g_recv, x_send, x_recv, own_sem,
):
    x, y, z, k = positions()
    me, slab, row = z * 2 + k, z // 2, z % 2 * 2 + k
    n_chunk = 8
    chunk = p_ref.shape[0] // n_chunk

    def p_copy(n):
        rows = pl.ds(n * chunk, chunk)
        return pltpu.make_async_copy(p_ref.at[rows], stage.at[rows], p_sem.at[n])

    d_copy = pltpu.make_async_copy(d_hbm, d_ref, in_sem.at[0])
    phase_copy = pltpu.make_async_copy(phase_hbm, phase_ref, in_sem.at[1])
    segment_copy = pltpu.make_async_copy(segment_hbm, segment_ref, in_sem.at[2])
    d_copy.start()
    phase_copy.start()
    segment_copy.start()
    for n in range(n_chunk):
        p_copy(n).start()

    hops = (1, 3, 2)
    along_x = [device(x + d, y, z, k) for d in hops]
    along_y = [device(x, y + d, z, k) for d in hops]
    mates = [(0, 1), (1, 0), (1, 1), (3, 0), (3, 1), (2, 0), (2, 1)]
    barrier = pltpu.get_barrier_semaphore()
    partners = along_x + along_y + [device(x, y, z + dz, k + dk) for dz, dk in mates]
    for partner in partners:
        pl.semaphore_signal(barrier, inc=1, device_id=partner, device_id_type=MESH)

    d_copy.wait()
    for h in range(2):
        low = d_ref[:, h * 1024:(h + 1) * 1024].astype(jnp.float32)
        high = d_ref[:, 2048 + h * 1024:2048 + (h + 1) * 1024].astype(jnp.float32)
        d_all[h, x, y] = jnp.concatenate([low, high], 0).astype(jnp.bfloat16)
    pl.semaphore_wait(barrier, len(partners))

    axes = (along_x, along_y)

    def send_block(h, block_x, block_y, line, n):
        block = d_all.at[h, block_x, block_y]
        copies = [remote(block, block, d_send.at[h, n + i], d_recv.at[h, n + i], line[i]) for i in range(3)]
        for copy in copies:
            copy.start()
        return copies

    first = [send_block(h, x, y, axes[h], 0) for h in range(2)]
    second = [copy for h in range(2) for copy in send_block(h, x, y, axes[1 - h], 3)]
    for i, hop in enumerate(hops):
        for h in range(2):
            first[h][i].wait_recv()
            from_x, from_y = ((x - hop) % 4, y) if h == 0 else (x, (y - hop) % 4)
            second += send_block(h, from_x, from_y, axes[1 - h], 6 + 3 * i)
    first = first[0] + first[1]

    to = lax.broadcasted_iota(jnp.int32, (256, 256), 0)
    source = lax.broadcasted_iota(jnp.int32, (256, 256), 1)
    permute = jnp.where((to % 32) * 8 + to // 32 == source, 1.0, 0.0).astype(jnp.bfloat16)

    def sort_rows(n):
        rows = stage[pl.ds(pl.multiple_of(n * 1024, 1024), 1024), :]
        wide = jnp.concatenate([rows[q * 256:(q + 1) * 256] for q in range(4)], 1)
        out = jnp.dot(permute, wide, preferred_element_type=jnp.float32).astype(jnp.bfloat16)
        for a in range(4):
            for b in range(2):
                part = out[(a * 2 + b) * 32:(a * 2 + b + 1) * 32]
                lanes = slice(a % 2 * 128, a % 2 * 128 + 128)
                for q in range(4):
                    at = pl.ds(pl.multiple_of(n * 128 + q * 32, 32), 32)
                    planes[b * 2 + a // 2, at, lanes] = part[:, q * 128:(q + 1) * 128]

    def sort_chunk(n, _):
        p_copy(n).wait()
        for i in range(4):
            sort_rows(n * 4 + i)
        return 0

    lax.fori_loop(0, n_chunk, sort_chunk, 0)
    phase_copy.wait()
    segment_copy.wait()
    for copy in second:
        copy.wait_recv()
    for h in range(2):
        for q in range(2):
            part = d_all[h].astype(jnp.float32).reshape(16, 16, 1024)[:, q * 8:(q + 1) * 8, :]
            at = q * 2048 + h * 1024
            d_rows[:, at:at + 1024] = part.reshape(128, 1024).astype(jnp.bfloat16)

    def features(b):
        for p in range(2):
            angles = jnp.dot(d_rows[...], planes[b * 2 + p], preferred_element_type=jnp.float32)
            for i in range(2):
                a = p * 2 + i
                value = cosine(angles[:, i * 128:(i + 1) * 128] + phase_ref[a, b:b + 1])
                natural[b, a] = value.astype(jnp.bfloat16)
                turned[a, b * 4:(b + 1) * 4] = value.T.astype(jnp.bfloat16).reshape(4, 2, 16, 128)

    batches = [(pl.ds(0, 1), None), (pl.ds(1, 2), pl.ds(2, 2)), (pl.ds(3, 4), pl.ds(4, 4))]
    shares = []
    for n, (slots, chunks) in enumerate(batches):
        for i, (dz, dk) in enumerate(mates):
            j = mates.index((-dz % 4, dk))
            z2, k2 = (z + dz) % 4, (k + dk) % 2
            theirs = pl.ds(z2 // 2, 1) if chunks is None else chunks
            group = (me - (z2 * 2 + k2) + 8) % 8
            shares.append(remote(
                turned.at[z2 % 2 * 2 + k2, theirs], left_ref.at[slots, :, x, y, group],
                e_send.at[n, i], e_recv.at[n, j], device(x, y, z2, k2)))
    own_right = pltpu.make_async_copy(natural.at[slab], right_ref.at[me], own_sem)
    mate = device(x, y, z, k + 1)
    rights = []
    for i, dz in enumerate(hops):
        target = device(x, y, z + dz, k)
        rights.append(remote(
            natural.at[(z + dz) % 4 // 2], right_ref.at[me], r_send.at[i], r_recv.at[hops.index(-dz % 4)], target))
    rights.append(remote(natural.at[slab], right_ref.at[me], r_send.at[3], r_recv.at[3], mate))
    handed = []
    for i, dz in enumerate(hops):
        at = right_ref.at[(z + dz) % 4 * 2 + k]
        handed.append(remote(at, at, r_send.at[4 + i], r_recv.at[4 + i], mate))

    features(0)
    for copy in shares[:14]:
        copy.start()
    features(1)
    left_ref[0, :, x, y, 0] = turned[row, slab]
    left_ref[1:7, :, x, y, 0] = turned[row, 2:8]

    px, mx, py, my = along_x[0], along_x[1], along_y[0], along_y[1]
    xp, xm, yp, ym = (x + 1) % 4, (x + 3) % 4, (y + 1) % 4, (y + 3) % 4

    def copies(slot, number):
        if slot is OWN:
            def part(h, at_x, at_y, half=None):
                slots = {None: pl.ds(0, 7), 0: pl.ds(0, 4), 1: pl.ds(4, 3)}[half]
                return left_ref.at[slots, h, at_x, at_y, 0]
        else:
            def part(h, at_x, at_y, half=None):
                groups = {None: pl.ds(1, 7), 0: pl.ds(1, 3), 1: pl.ds(4, 4)}[half]
                return left_ref.at[slot, h, at_x, at_y, groups]
        low, high = pl.ds(0, 2), pl.ds(2, 2)
        if number == 0:
            pairs = [(part(0, x, y), px), (part(0, x, y), mx), (part(1, x, y), py), (part(1, x, y), my)]
        elif number == 1:
            pairs = [(part(0, xm, y, 0), px), (part(0, xp, y, 1), mx), (part(1, x, ym, 0), py), (part(1, x, yp, 1), my)]
        elif number == 2:
            pairs = [(part(0, low, y), py), (part(0, high, y), my), (part(1, x, low), px), (part(1, x, high), mx)]
        elif number == 3:
            pairs = [(part(0, low, ym), py), (part(0, high, yp), my), (part(1, xm, low), px), (part(1, xp, high), mx)]
        else:
            pairs = [(part(0, high, y), py), (part(0, low, y), my), (part(1, x, high), px), (part(1, x, low), mx)]
        at = 7 if slot is OWN else slot
        return [
            remote(ref, ref, g_send.at[at, number, i], g_recv.at[at, number, i], target)
            for i, (ref, target) in enumerate(pairs)
        ]

    def crossing(h, half):
        return remote(
            left_ref.at[0, h, :, :, pl.ds(half * 4, 4)], left_ref.at[7, h, :, :, pl.ds(4 - half * 4, 4)],
            x_send.at[h, half], x_recv.at[h, half], device(x, y, z + 2, k))

    crossings = [crossing(h, half) for h in range(2) for half in range(2)]

    def wait_shares(n):
        for copy in shares[n * 7:(n + 1) * 7]:
            copy.wait_recv()

    def multiply(slot, number):
        b, quarter = number // 4, number % 4
        rows = chunk_rows(left_ref, slot)
        for out_ref, at, factor in ((instant_ref, 0, 1.0 / 1024), (lagged_ref, 512, scale[0])):
            total = jnp.dot(rows, columns[:, at:at + 512], preferred_element_type=jnp.float32) * factor
            for c in range(16):
                for a in range(4):
                    part = total[c * 32:(c + 1) * 32, a * 128:(a + 1) * 128]
                    out_ref[b, c, quarter, pl.ds(a, 32, stride=4), :] = part

    def advance(slot, number):
        if number < 5:
            if number > 0:
                for copy in copies(slot, number - 1):
                    copy.wait_recv()
            elif slot is not OWN:
                for n, at in enumerate((0, 1, 3)):
                    pl.when(slot == at)(functools.partial(wait_shares, n))
            for sent in (2, 4) if number == 2 else (number,):
                for copy in copies(slot, sent):
                    copy.start()
            return
        for sent in (4, 3):
            for copy in copies(slot, sent):
                copy.wait_recv()
        if slot is not OWN:
            @pl.when(slot == 0)
            def _():
                for copy in crossings:
                    copy.start()

        for sent in range(5):
            for copy in copies(slot, sent):
                copy.wait_send()

    def rounds(step, _):
        for number, lead in ((0, 0), (1, 1), (2, 2), (3, 3), (5, 4)):
            slot = step - lead - 1
            pl.when(slot == -1)(functools.partial(advance, OWN, number))
            pl.when(jnp.logical_and(slot >= 0, slot < 7))(functools.partial(advance, slot, number))
        return 0

    def job(n, _):
        slot = n + jnp.where(n == 5, 2, 0) - jnp.where(n == 6, 1, 0)

        @pl.when(n == 5)
        def _():
            for copy in crossings:
                copy.wait_recv()

        multiply(slot, jnp.where(slot == 7, 1 - slab, jnp.where(slot == 0, slab, slot + 1)))
        return 0

    def later(step, _):
        rounds(step, 0)
        begin = jnp.minimum(2 * (step - 7), 5)
        end = jnp.where(step == 10, 7, jnp.minimum(2 * (step - 6), 5))
        lax.fori_loop(begin, end, job, 0)
        return 0

    lax.fori_loop(0, 1, rounds, 0)
    for copy in shares[14:] + rights:
        copy.start()
    own_right.start()
    lax.fori_loop(1, 6, rounds, 0)
    for copy in rights[:3]:
        copy.wait_recv()
    for copy in handed:
        copy.start()
    lax.fori_loop(6, 7, rounds, 0)
    own_right.wait()
    rights[3].wait_recv()
    for copy in handed:
        copy.wait_recv()
    right_columns(right_ref, segment_ref, columns, scale, me)
    for copy in first + second + shares + rights + handed:
        copy.wait_send()
    lax.fori_loop(7, 11, later, 0)
    for copy in crossings:
        copy.wait_send()
    lax.fori_loop(11, 12, rounds, 0)


def chunk_rows(left_ref, slot):
    return jnp.concatenate(
        [
            jnp.concatenate([left_ref[slot, h, x, y, g] for g in range(8)], 1)
            for x in range(4) for y in range(4) for h in range(2)
        ],
        0,
    )


def paired_before(segment_ref):
    ids = jnp.broadcast_to(segment_ref[...], (8, 1024))
    frame = lax.broadcasted_iota(jnp.int32, (8, 1024), 1)
    return jnp.where((pltpu.roll(ids, LAG, 1) == ids) & (frame >= LAG), 1.0, 0.0)[0:1]


def right_columns(right_ref, segment_ref, columns, scale, me):
    paired = paired_before(segment_ref)
    scale[0] = 1.0 / jnp.sum(paired)

    def wide(g):
        return jnp.concatenate([right_ref[g, a] for a in range(4)], 1)

    for n in range(8):
        at = pl.ds(pl.multiple_of((n - me + 8) % 8 * 128, 128), 128)
        columns[at, 0:512] = wide(n)
        g = min(n, 6)
        here = lax.broadcasted_iota(jnp.int32, (128, 256), 0) + n * 128
        there = lax.broadcasted_iota(jnp.int32, (128, 256), 1) + g * 128
        take = jnp.where(there == here + LAG, paired[:, g * 128:g * 128 + 256], 0.0).astype(jnp.bfloat16)
        both = jnp.concatenate([wide(g), wide(g + 1)], 0)
        columns[at, 512:1024] = jnp.dot(take, both, preferred_element_type=jnp.float32).astype(jnp.bfloat16)


OWN = "own"
TILES = (2, 16, 4, 128, 128)


def gather(distances, projection, phases, segment_ids):
    bf16, f32 = jnp.bfloat16, jnp.float32
    dma = pltpu.SemaphoreType.DMA
    anywhere = pl.BlockSpec(memory_space=pl.ANY)
    vmem = pl.BlockSpec(memory_space=pltpu.VMEM)
    return pl.pallas_call(
        gather_kernel,
        out_shape=(
            pltpu.VMEM(TILES, f32),
            pltpu.VMEM(TILES, f32),
            pltpu.VMEM((8, 2, 4, 4, 8, 16, 128), bf16),
            pltpu.VMEM((1024, 1024), bf16),
        ),
        in_specs=[anywhere] * 4,
        out_specs=(vmem,) * 4,
        scratch_shapes=[
            pltpu.VMEM((8, 4096), bf16),
            pltpu.VMEM((4, 2, 128), f32),
            pltpu.VMEM((1, 1024), jnp.int32),
            pltpu.VMEM((32768, 128), bf16),
            pltpu.VMEM((4, 4096, 256), bf16),
            pltpu.VMEM((2, 4, 4, 16, 1024), bf16),
            pltpu.VMEM((128, 4096), bf16),
            pltpu.VMEM((2, 4, 128, 128), bf16),
            pltpu.VMEM((4, 8, 2, 16, 128), bf16),
            pltpu.VMEM((8, 4, 128, 128), bf16),
            pltpu.SMEM((1,), f32),
            dma((3,)),
            dma((8,)),
            dma((2, 15)),
            dma((2, 15)),
            dma((3, 7)),
            dma((3, 7)),
            dma((7,)),
            dma((7,)),
            dma((8, 5, 4)),
            dma((8, 5, 4)),
            dma((2, 2)),
            dma((2, 2)),
            dma,
        ],
        compiler_params=pltpu.CompilerParams(
            collective_id=0, has_side_effects=True, vmem_limit_bytes=36 * MIB
        ),
        name="gather_features",
    )(distances, projection, phases, segment_ids)


LAST_SLOT, LAST_CHUNK = 6, 7


def finish_kernel(
    instant_tiles, lagged_tiles, left_ref, columns, segment_ref, instant_ref, lagged_ref, instant_last, lagged_last, sem
):
    copies = []

    def move(source, target, n):
        copy = pltpu.make_async_copy(source, target, sem.at[n])
        copy.start()
        copies.append(copy)

    outs = ((instant_tiles, instant_ref, instant_last), (lagged_tiles, lagged_ref, lagged_last))
    for i, (tiles, out_ref, _) in enumerate(outs):
        move(tiles.at[0], out_ref.at[0], i * 3)
        move(tiles.at[1, :, pl.ds(0, 3)], out_ref.at[1, :, pl.ds(0, 3)], i * 3 + 1)
    rows = chunk_rows(left_ref, LAST_SLOT)
    inverse = 1.0 / jnp.sum(paired_before(segment_ref))
    for i, (_, out_ref, last) in enumerate(outs):
        total = jnp.dot(rows, columns[:, i * 512:(i + 1) * 512], preferred_element_type=jnp.float32)
        total = total * (inverse if i else 1.0 / 1024)
        for c in range(16):
            for a in range(4):
                last[c, pl.ds(a, 32, stride=4), :] = total[c * 32:(c + 1) * 32, a * 128:(a + 1) * 128]
        move(last, out_ref.at[1, :, 3], i * 3 + 2)
    for copy in copies:
        copy.wait()


def finish(tiles, segment_ids):
    out = jax.ShapeDtypeStruct(TILES, jnp.float32)
    vmem = pl.BlockSpec(memory_space=pltpu.VMEM)
    anywhere = pl.BlockSpec(memory_space=pl.ANY)
    return pl.pallas_call(
        finish_kernel,
        out_shape=(out, out),
        in_specs=[vmem] * 5,
        out_specs=(anywhere, anywhere),
        scratch_shapes=[
            pltpu.VMEM((16, 128, 128), jnp.float32),
            pltpu.VMEM((16, 128, 128), jnp.float32),
            pltpu.SemaphoreType.DMA((6,)),
        ],
        compiler_params=pltpu.CompilerParams(vmem_limit_bytes=4 * MIB),
        name="covariances",
    )(*tiles, segment_ids)


def per_device(distances, projection, phases, segment_ids):
    segments = segment_ids.reshape(1, 1024)
    tiles = gather(distances, projection.reshape(32768, 128), phases, segments)
    tiles = [pltpu.with_memory_space_constraint(part, pltpu.VMEM) for part in tiles]
    instant, lagged = finish(tiles, segments)
    return instant.reshape(4096, 4, 1, 128), lagged.reshape(4096, 4, 1, 128)


def solution(mesh):
    placed = (
        P(("slab", "row", "col"), None),
        P(None, None, None, "col"),
        P(None, None, "col"),
        P(),
    )
    return jax.shard_map(
        per_device,
        mesh=mesh,
        in_specs=placed,
        out_specs=(P("row", None, "slab", "col"), P("row", None, "slab", "col")),
        check_vma=False,
    )
```

```python
import functools

import jax
import jax.numpy as jnp
from jax import lax
from jax.experimental import pallas as pl
from jax.experimental.pallas import tpu as pltpu
from jax.sharding import PartitionSpec as P

LAG = 50
MESH = pl.DeviceIdType.MESH
MIB = 1 << 20
PI_A, PI_B, PI_C = 3.140625, 0.0009670257568359375, 6.2771141529083252e-07
COS_POLY = (
    2.08767570e-09, -2.75573192e-07, 2.48015873e-05, -1.38888889e-03, 4.16666667e-02, -0.5, 1.0
)


def cosine(angle):
    k = jnp.floor(angle * (1.0 / 3.14159265358979) + 0.5)
    r = ((angle - k * PI_A) - k * PI_B) - k * PI_C
    odd = k - 2.0 * jnp.floor(k * 0.5)
    square = r * r
    value = jnp.full_like(square, COS_POLY[0])
    for term in COS_POLY[1:]:
        value = value * square + term
    return value * (1.0 - 2.0 * odd)


def positions():
    slab, row, col = lax.axis_index("slab"), lax.axis_index("row"), lax.axis_index("col")
    return col // 4, col % 4, slab * 2 + row // 2, row % 2


def device(x, y, z, k):
    x, y, z, k = x % 4, y % 4, z % 4, k % 2
    return (z // 2, (z % 2) * 2 + k, x * 4 + y)


def remote(src, dst, send, recv, target):
    return pltpu.make_async_remote_copy(
        src_ref=src, dst_ref=dst, send_sem=send, recv_sem=recv, device_id=target, device_id_type=MESH
    )


def taken(view, sem):
    pltpu.make_async_copy(view, view, sem).wait()


def gather_kernel(
    d_hbm, p_ref, phase_hbm, segment_hbm, instant_ref, lagged_ref, left_ref, columns,
    phase_ref, segment_ref, stage, planes, d_all, d_rows, natural, turned, right_ref, scale,
    in_sem, p_sem, d_sem, first_recv, e_send, e_recv, r_sem, g_send, g_recv, x_sem, own_sem,
):
    x, y, z, k = positions()
    me, slab, row = z * 2 + k, z // 2, z % 2 * 2 + k
    n_chunk = 4
    chunk = p_ref.shape[0] // n_chunk

    def p_copy(n):
        rows = pl.ds(n * chunk, chunk)
        return pltpu.make_async_copy(p_ref.at[rows], stage.at[rows], p_sem.at[n])

    phase_copy = pltpu.make_async_copy(phase_hbm, phase_ref, in_sem.at[0])
    segment_copy = pltpu.make_async_copy(segment_hbm, segment_ref, in_sem.at[1])
    own_depth = [d_hbm.at[:, pl.ds(h * 2048, 2048)] for h in range(2)]
    d_copies = [pltpu.make_async_copy(own_depth[h], d_all.at[h, x, y], in_sem.at[2]) for h in range(2)]
    for copy in d_copies + [phase_copy, segment_copy]:
        copy.start()
    for n in range(n_chunk):
        p_copy(n).start()

    hops = (1, 3, 2)
    along_x = [device(x + d, y, z, k) for d in hops]
    along_y = [device(x, y + d, z, k) for d in hops]
    mates = [(0, 1), (1, 0), (1, 1), (3, 0), (3, 1), (2, 0), (2, 1)]
    barrier = pltpu.get_barrier_semaphore()
    partners = along_x + along_y + [device(x, y, z + dz, k + dk) for dz, dk in mates]
    for partner in partners:
        pl.semaphore_signal(barrier, inc=1, device_id=partner, device_id_type=MESH)

    pl.semaphore_wait(barrier, len(partners))

    axes = (along_x, along_y)

    def send_block(h, source, block, line, recv):
        for i in range(3):
            remote(source, block, d_sem.at[0 if recv is None else 1], d_sem.at[2] if recv is None else recv(h, i), line[i]).start()

    for h in range(2):
        send_block(h, own_depth[h], d_all.at[h, x, y], axes[h], lambda h, i: first_recv.at[h, i])
    for h in range(2):
        send_block(h, own_depth[h], d_all.at[h, x, y], axes[1 - h], None)
    for i, hop in enumerate(hops):
        for h in range(2):
            from_x, from_y = ((x - hop) % 4, y) if h == 0 else (x, (y - hop) % 4)
            block = d_all.at[h, from_x, from_y]
            taken(block, first_recv.at[h, i])
            send_block(h, block, block, axes[1 - h], None)

    to = lax.broadcasted_iota(jnp.int32, (256, 256), 0)
    source = lax.broadcasted_iota(jnp.int32, (256, 256), 1)
    permute = jnp.where((to % 32) * 8 + to // 32 == source, 1.0, 0.0).astype(jnp.bfloat16)

    def sort_rows(n):
        rows = stage[pl.ds(pl.multiple_of(n * 1024, 1024), 1024), :]
        wide = jnp.concatenate([rows[q * 256:(q + 1) * 256] for q in range(4)], 1)
        out = jnp.dot(permute, wide, preferred_element_type=jnp.float32).astype(jnp.bfloat16)
        for a in range(4):
            for b in range(2):
                part = out[(a * 2 + b) * 32:(a * 2 + b + 1) * 32]
                lanes = slice(a % 2 * 128, a % 2 * 128 + 128)
                for q in range(4):
                    at = pl.ds(pl.multiple_of(n * 128 + q * 32, 32), 32)
                    planes[b * 2 + a // 2, at, lanes] = part[:, q * 128:(q + 1) * 128]

    def sort_chunk(n, _):
        p_copy(n).wait()
        for i in range(8):
            sort_rows(n * 8 + i)
        return 0

    lax.fori_loop(0, n_chunk, sort_chunk, 0)
    phase_copy.wait()
    segment_copy.wait()
    taken(d_all.at[:, 0:3], d_sem.at[2])
    taken(d_all.at[:, x, y], in_sem.at[2])
    for h in range(2):
        part = d_all[h].astype(jnp.float32).reshape(128, 2048)
        d_rows[:, h * 2048:(h + 1) * 2048] = part.astype(jnp.bfloat16)

    def features(b):
        for p in range(2):
            angles = jnp.dot(d_rows[...], planes[b * 2 + p], preferred_element_type=jnp.float32)
            for i in range(2):
                a = p * 2 + i
                value = cosine(angles[:, i * 128:(i + 1) * 128] + phase_ref[a, b:b + 1])
                natural[b, a] = value.astype(jnp.bfloat16)
                turned[a, b * 4:(b + 1) * 4] = value.T.astype(jnp.bfloat16).reshape(4, 2, 16, 128)

    batches = [(pl.ds(0, 1), None), (pl.ds(1, 2), pl.ds(2, 2)), (pl.ds(3, 4), pl.ds(4, 4))]
    shares = []
    for n, (slots, chunks) in enumerate(batches):
        for i, (dz, dk) in enumerate(mates):
            z2, k2 = (z + dz) % 4, (k + dk) % 2
            theirs = pl.ds(z2 // 2, 1) if chunks is None else chunks
            group = (me - (z2 * 2 + k2) + 8) % 8
            shares.append(remote(
                turned.at[z2 % 2 * 2 + k2, theirs], left_ref.at[slots, :, x, y, group],
                e_send.at[n], e_recv.at[n], device(x, y, z2, k2)))
    own_right = pltpu.make_async_copy(natural.at[slab], right_ref.at[me], own_sem)
    mate = device(x, y, z, k + 1)
    rights = []
    for i, dz in enumerate(hops):
        target = device(x, y, z + dz, k)
        rights.append(remote(natural.at[(z + dz) % 4 // 2], right_ref.at[me], r_sem.at[0], r_sem.at[1], target))
    rights.append(remote(natural.at[slab], right_ref.at[me], r_sem.at[0], r_sem.at[2], mate))
    handed = []
    for i, dz in enumerate(hops):
        at = right_ref.at[(z + dz) % 4 * 2 + k]
        handed.append(remote(at, at, r_sem.at[3], r_sem.at[2], mate))

    features(0)
    for copy in shares[:14]:
        copy.start()
    features(1)
    left_ref[0, :, x, y, 0] = turned[row, slab]
    left_ref[1:7, :, x, y, 0] = turned[row, 2:8]

    px, mx, py, my = along_x[0], along_x[1], along_y[0], along_y[1]
    xp, xm, yp, ym = (x + 1) % 4, (x + 3) % 4, (y + 1) % 4, (y + 3) % 4

    def copies(slot, number):
        if slot is OWN:
            def part(h, at_x, at_y, half=None):
                slots = {None: pl.ds(0, 7), 0: pl.ds(0, 4), 1: pl.ds(4, 3)}[half]
                return left_ref.at[slots, h, at_x, at_y, 0]
        else:
            def part(h, at_x, at_y, half=None):
                groups = {None: pl.ds(1, 7), 0: pl.ds(1, 3), 1: pl.ds(4, 4)}[half]
                return left_ref.at[slot, h, at_x, at_y, groups]
        low, high = pl.ds(0, 2), pl.ds(2, 2)
        if number == 0:
            pairs = [(part(0, x, y), px), (part(0, x, y), mx), (part(1, x, y), py), (part(1, x, y), my)]
        elif number == 1:
            pairs = [(part(0, xm, y, 0), px), (part(0, xp, y, 1), mx), (part(1, x, ym, 0), py), (part(1, x, yp, 1), my)]
        elif number == 2:
            pairs = [(part(0, low, y), py), (part(0, high, y), my), (part(1, x, low), px), (part(1, x, high), mx)]
        elif number == 3:
            pairs = [(part(0, low, ym), py), (part(0, high, yp), my), (part(1, xm, low), px), (part(1, xp, high), mx)]
        else:
            pairs = [(part(0, high, y), py), (part(0, low, y), my), (part(1, x, high), px), (part(1, x, low), mx)]
        place = order(slot)
        send, recv = g_send.at[place % 2, number], g_recv.at[place, number]
        return [remote(ref, ref, send, recv, target) for ref, target in pairs]

    def order(slot):
        return 0 if slot is OWN else slot + 1

    def whole(number):
        blocks = left_ref.at[0, 0, :, :, pl.ds(1, 7)]
        return (blocks.at[0], blocks.at[0, 0:2], blocks.at[0:2], blocks.at[0:2], blocks.at[0:2])[number]

    def received(slot, number):
        taken(whole(number), g_recv.at[order(slot), number])

    def crossing(h, half):
        return remote(
            left_ref.at[0, h, :, :, pl.ds(half * 4, 4)], left_ref.at[7, h, :, :, pl.ds(4 - half * 4, 4)],
            x_sem.at[0], x_sem.at[1], device(x, y, z + 2, k))

    crossings = [crossing(h, half) for h in range(2) for half in range(2)]

    def exchanged(n):
        return left_ref.at[batches[n][0], :, x, y, pl.ds(1, 7)]

    def wait_shares(n):
        taken(exchanged(n), e_recv.at[n])

    def multiply(slot, number):
        b, quarter = number // 4, number % 4
        rows = chunk_rows(left_ref, slot)
        for out_ref, at, factor in ((instant_ref, 0, 1.0 / 1024), (lagged_ref, 512, scale[0])):
            total = jnp.dot(rows, columns[:, at:at + 512], preferred_element_type=jnp.float32) * factor
            for c in range(16):
                for a in range(4):
                    part = total[c * 32:(c + 1) * 32, a * 128:(a + 1) * 128]
                    out_ref[b, c, quarter, pl.ds(a, 32, stride=4), :] = part

    def advance(slot, number):
        if number < 5:
            if number > 0:
                received(slot, number - 1)
            elif slot is not OWN:
                for n, at in enumerate((0, 1, 3)):
                    pl.when(slot == at)(functools.partial(wait_shares, n))
            for sent in (2, 4) if number == 2 else (number,):
                if slot is not OWN:
                    @pl.when(slot >= 1)
                    def _():
                        taken(whole(sent), g_send.at[order(slot) % 2, sent])

                for copy in copies(slot, sent):
                    copy.start()
            return
        for sent in (4, 3):
            received(slot, sent)
        if slot is not OWN:
            @pl.when(slot == 0)
            def _():
                for copy in crossings:
                    copy.start()

    def rounds(numbers, step, _):
        for number in numbers:
            slot = step - min(number, 4) - 1
            pl.when(slot == -1)(functools.partial(advance, OWN, number))
            pl.when(jnp.logical_and(slot >= 0, slot < 7))(functools.partial(advance, slot, number))
        return 0

    early = functools.partial(rounds, (1, 0, 2, 3))
    steady = functools.partial(rounds, (0, 1, 2, 3, 5))

    def job(n, _):
        slot = n + jnp.where(n == 5, 2, 0) - jnp.where(n == 6, 1, 0)

        @pl.when(n == 5)
        def _():
            taken(left_ref.at[7], x_sem.at[1])

        multiply(slot, jnp.where(slot == 7, 1 - slab, jnp.where(slot == 0, slab, slot + 1)))
        return 0

    def later(step, _):
        steady(step, 0)
        begin = step - 6 + jnp.where(step >= 8, 1, 0)
        end = step - 5 + jnp.where(step >= 7, 1, 0) + jnp.where(step == 10, 1, 0)
        lax.fori_loop(begin, end, job, 0)
        return 0

    lax.fori_loop(0, 1, early, 0)
    for copy in shares[14:] + rights:
        copy.start()
    own_right.start()
    lax.fori_loop(1, 4, early, 0)
    lax.fori_loop(4, 5, steady, 0)
    taken(right_ref.at[0:3], r_sem.at[1])
    for copy in handed:
        copy.start()
    lax.fori_loop(5, 6, steady, 0)
    own_right.wait()
    taken(right_ref.at[0:4], r_sem.at[2])
    right_columns(right_ref, segment_ref, columns, scale, me)
    taken(d_all.at[:, 0, 0:3], d_sem.at[1])
    taken(d_all.at[:, 0:3], d_sem.at[0])
    for n in range(3):
        taken(exchanged(n), e_send.at[n])
    taken(right_ref.at[0:4], r_sem.at[0])
    taken(right_ref.at[0:3], r_sem.at[3])
    lax.fori_loop(6, 11, later, 0)
    taken(left_ref.at[7], x_sem.at[0])
    lax.fori_loop(11, 12, steady, 0)
    for place in range(2):
        for number in range(5):
            taken(whole(number), g_send.at[place, number])


def chunk_rows(left_ref, slot):
    return jnp.concatenate(
        [
            jnp.concatenate([left_ref[slot, h, x, y, g] for g in range(8)], 1)
            for x in range(4) for y in range(4) for h in range(2)
        ],
        0,
    )


def paired_before(segment_ref):
    ids = jnp.broadcast_to(segment_ref[...], (8, 1024))
    frame = lax.broadcasted_iota(jnp.int32, (8, 1024), 1)
    return jnp.where((pltpu.roll(ids, LAG, 1) == ids) & (frame >= LAG), 1.0, 0.0)[0:1]


def right_columns(right_ref, segment_ref, columns, scale, me):
    paired = paired_before(segment_ref)
    scale[0] = 1.0 / jnp.sum(paired)

    def wide(g):
        return jnp.concatenate([right_ref[g, a] for a in range(4)], 1)

    for n in range(8):
        at = pl.ds(pl.multiple_of((n - me + 8) % 8 * 128, 128), 128)
        columns[at, 0:512] = wide(n)
        g = min(n, 6)
        here = lax.broadcasted_iota(jnp.int32, (128, 256), 0) + n * 128
        there = lax.broadcasted_iota(jnp.int32, (128, 256), 1) + g * 128
        take = jnp.where(there == here + LAG, paired[:, g * 128:g * 128 + 256], 0.0).astype(jnp.bfloat16)
        both = jnp.concatenate([wide(g), wide(g + 1)], 0)
        columns[at, 512:1024] = jnp.dot(take, both, preferred_element_type=jnp.float32).astype(jnp.bfloat16)


OWN = "own"
TILES = (2, 16, 4, 128, 128)


def gather(distances, projection, phases, segment_ids):
    bf16, f32 = jnp.bfloat16, jnp.float32
    dma = pltpu.SemaphoreType.DMA
    anywhere = pl.BlockSpec(memory_space=pl.ANY)
    vmem = pl.BlockSpec(memory_space=pltpu.VMEM)
    return pl.pallas_call(
        gather_kernel,
        out_shape=(
            pltpu.VMEM(TILES, f32),
            pltpu.VMEM(TILES, f32),
            pltpu.VMEM((8, 2, 4, 4, 8, 16, 128), bf16),
            pltpu.VMEM((1024, 1024), bf16),
        ),
        in_specs=[anywhere] * 4,
        out_specs=(vmem,) * 4,
        scratch_shapes=[
            pltpu.VMEM((4, 2, 128), f32),
            pltpu.VMEM((1, 1024), jnp.int32),
            pltpu.VMEM((32768, 128), bf16),
            pltpu.VMEM((4, 4096, 256), bf16),
            pltpu.VMEM((2, 4, 4, 8, 2048), bf16),
            pltpu.VMEM((128, 4096), bf16),
            pltpu.VMEM((2, 4, 128, 128), bf16),
            pltpu.VMEM((4, 8, 2, 16, 128), bf16),
            pltpu.VMEM((8, 4, 128, 128), bf16),
            pltpu.SMEM((1,), f32),
            dma((3,)),
            dma((4,)),
            dma((3,)),
            dma((2, 3)),
            dma((3,)),
            dma((3,)),
            dma((4,)),
            dma((2, 5)),
            dma((8, 5)),
            dma((2,)),
            dma,
        ],
        compiler_params=pltpu.CompilerParams(
            collective_id=0, has_side_effects=True, vmem_limit_bytes=36 * MIB
        ),
        name="gather_features",
    )(distances, projection, phases, segment_ids)


LAST_SLOT, LAST_CHUNK = 6, 7


def finish_kernel(
    instant_tiles, lagged_tiles, left_ref, columns, segment_ref, instant_ref, lagged_ref, instant_last, lagged_last, sem
):
    copies = []

    def move(source, target, n):
        copy = pltpu.make_async_copy(source, target, sem.at[n])
        copy.start()
        copies.append(copy)

    outs = ((instant_tiles, instant_ref, instant_last), (lagged_tiles, lagged_ref, lagged_last))
    for i, (tiles, out_ref, _) in enumerate(outs):
        move(tiles.at[0], out_ref.at[0], i * 3)
        move(tiles.at[1, :, pl.ds(0, 3)], out_ref.at[1, :, pl.ds(0, 3)], i * 3 + 1)
    rows = chunk_rows(left_ref, LAST_SLOT)
    inverse = 1.0 / jnp.sum(paired_before(segment_ref))
    for i, (_, out_ref, last) in enumerate(outs):
        total = jnp.dot(rows, columns[:, i * 512:(i + 1) * 512], preferred_element_type=jnp.float32)
        total = total * (inverse if i else 1.0 / 1024)
        for c in range(16):
            for a in range(4):
                last[c, pl.ds(a, 32, stride=4), :] = total[c * 32:(c + 1) * 32, a * 128:(a + 1) * 128]
        move(last, out_ref.at[1, :, 3], i * 3 + 2)
    for copy in copies:
        copy.wait()


def finish(tiles, segment_ids):
    out = jax.ShapeDtypeStruct(TILES, jnp.float32)
    vmem = pl.BlockSpec(memory_space=pltpu.VMEM)
    anywhere = pl.BlockSpec(memory_space=pl.ANY)
    return pl.pallas_call(
        finish_kernel,
        out_shape=(out, out),
        in_specs=[vmem] * 5,
        out_specs=(anywhere, anywhere),
        scratch_shapes=[
            pltpu.VMEM((16, 128, 128), jnp.float32),
            pltpu.VMEM((16, 128, 128), jnp.float32),
            pltpu.SemaphoreType.DMA((6,)),
        ],
        compiler_params=pltpu.CompilerParams(vmem_limit_bytes=4 * MIB),
        name="covariances",
    )(*tiles, segment_ids)


def per_device(distances, projection, phases, segment_ids):
    segments = segment_ids.reshape(1, 1024)
    tiles = gather(distances, projection.reshape(32768, 128), phases, segments)
    tiles = [pltpu.with_memory_space_constraint(part, pltpu.VMEM) for part in tiles]
    instant, lagged = finish(tiles, segments)
    return instant.reshape(4096, 4, 1, 128), lagged.reshape(4096, 4, 1, 128)


def solution(mesh):
    placed = (
        P(("slab", "row", "col"), None),
        P(None, None, None, "col"),
        P(None, None, "col"),
        P(),
    )
    return jax.shard_map(
        per_device,
        mesh=mesh,
        in_specs=placed,
        out_specs=(P("row", None, "slab", "col"), P("row", None, "slab", "col")),
        check_vma=False,
    )
```

```python
import functools

import jax
import jax.numpy as jnp
from jax import lax
from jax.experimental import pallas as pl
from jax.experimental.pallas import tpu as pltpu
from jax.sharding import PartitionSpec as P

LAG = 50
MESH = pl.DeviceIdType.MESH
MIB = 1 << 20
PI_A, PI_B, PI_C = 3.140625, 0.0009670257568359375, 6.2771141529083252e-07
COS_POLY = (
    2.08767570e-09, -2.75573192e-07, 2.48015873e-05, -1.38888889e-03, 4.16666667e-02, -0.5, 1.0
)


def cosine(angle):
    k = jnp.floor(angle * (1.0 / 3.14159265358979) + 0.5)
    r = ((angle - k * PI_A) - k * PI_B) - k * PI_C
    odd = k - 2.0 * jnp.floor(k * 0.5)
    square = r * r
    value = jnp.full_like(square, COS_POLY[0])
    for term in COS_POLY[1:]:
        value = value * square + term
    return value * (1.0 - 2.0 * odd)


def positions():
    slab, row, col = lax.axis_index("slab"), lax.axis_index("row"), lax.axis_index("col")
    return col // 4, col % 4, slab * 2 + row // 2, row % 2


def device(x, y, z, k):
    x, y, z, k = x % 4, y % 4, z % 4, k % 2
    return (z // 2, (z % 2) * 2 + k, x * 4 + y)


def remote(src, dst, send, recv, target):
    return pltpu.make_async_remote_copy(
        src_ref=src, dst_ref=dst, send_sem=send, recv_sem=recv, device_id=target, device_id_type=MESH
    )


def taken(view, sem):
    pltpu.make_async_copy(view, view, sem).wait()


def gather_kernel(
    d_hbm, p_ref, phase_hbm, segment_hbm, instant_ref, lagged_ref, left_ref, columns,
    phase_ref, segment_ref, stage, planes, d_all, d_rows, natural, turned, right_ref, scale,
    in_sem, p_sem, d_sem, first_recv, e_send, e_recv, r_sem, g_send, g_recv, x_sem, own_sem,
):
    x, y, z, k = positions()
    me, slab, row = z * 2 + k, z // 2, z % 2 * 2 + k
    n_chunk = 4
    chunk = p_ref.shape[0] // n_chunk

    def p_copy(n):
        rows = pl.ds(n * chunk, chunk)
        return pltpu.make_async_copy(p_ref.at[rows], stage.at[rows], p_sem.at[n])

    phase_copy = pltpu.make_async_copy(phase_hbm, phase_ref, in_sem.at[0])
    segment_copy = pltpu.make_async_copy(segment_hbm, segment_ref, in_sem.at[1])
    own_depth = [d_hbm.at[:, pl.ds(h * 2048, 2048)] for h in range(2)]
    d_copies = [pltpu.make_async_copy(own_depth[h], d_all.at[h, x, y], in_sem.at[2]) for h in range(2)]
    for copy in d_copies + [phase_copy, segment_copy]:
        copy.start()
    for n in range(n_chunk):
        p_copy(n).start()

    hops = (1, 3, 2)
    along_x = [device(x + d, y, z, k) for d in hops]
    along_y = [device(x, y + d, z, k) for d in hops]
    mates = [(0, 1), (1, 0), (1, 1), (3, 0), (3, 1), (2, 0), (2, 1)]
    barrier = pltpu.get_barrier_semaphore()
    partners = along_x + along_y + [device(x, y, z + dz, k + dk) for dz, dk in mates]
    for partner in partners:
        pl.semaphore_signal(barrier, inc=1, device_id=partner, device_id_type=MESH)

    pl.semaphore_wait(barrier, len(partners))

    axes = (along_x, along_y)

    def send_block(h, source, block, line, recv):
        for i in range(3):
            remote(source, block, d_sem.at[0 if recv is None else 1], d_sem.at[2] if recv is None else recv(h, i), line[i]).start()

    for h in range(2):
        send_block(h, own_depth[h], d_all.at[h, x, y], axes[h], lambda h, i: first_recv.at[h, i])
    for h in range(2):
        send_block(h, own_depth[h], d_all.at[h, x, y], axes[1 - h], None)
    for i, hop in enumerate(hops):
        for h in range(2):
            from_x, from_y = ((x - hop) % 4, y) if h == 0 else (x, (y - hop) % 4)
            block = d_all.at[h, from_x, from_y]
            taken(block, first_recv.at[h, i])
            send_block(h, block, block, axes[1 - h], None)

    to = lax.broadcasted_iota(jnp.int32, (256, 256), 0)
    source = lax.broadcasted_iota(jnp.int32, (256, 256), 1)
    permute = jnp.where((to % 32) * 8 + to // 32 == source, 1.0, 0.0).astype(jnp.bfloat16)

    def sort_rows(n):
        rows = stage[pl.ds(pl.multiple_of(n * 1024, 1024), 1024), :]
        wide = jnp.concatenate([rows[q * 256:(q + 1) * 256] for q in range(4)], 1)
        out = jnp.dot(permute, wide, preferred_element_type=jnp.float32).astype(jnp.bfloat16)
        for a in range(4):
            for b in range(2):
                part = out[(a * 2 + b) * 32:(a * 2 + b + 1) * 32]
                lanes = slice(a % 2 * 128, a % 2 * 128 + 128)
                for q in range(4):
                    at = pl.ds(pl.multiple_of(n * 128 + q * 32, 32), 32)
                    planes[b * 2 + a // 2, at, lanes] = part[:, q * 128:(q + 1) * 128]

    def sort_chunk(n, _):
        p_copy(n).wait()
        for i in range(8):
            sort_rows(n * 8 + i)
        return 0

    lax.fori_loop(0, n_chunk, sort_chunk, 0)
    phase_copy.wait()
    segment_copy.wait()
    taken(d_all.at[:, 0:3], d_sem.at[2])
    taken(d_all.at[:, x, y], in_sem.at[2])
    for h in range(2):
        part = d_all[h].astype(jnp.float32).reshape(128, 2048)
        d_rows[:, h * 2048:(h + 1) * 2048] = part.astype(jnp.bfloat16)

    def features(b, p):
        angles = jnp.dot(d_rows[...], planes[b * 2 + p], preferred_element_type=jnp.float32)
        for i in range(2):
            a = p * 2 + i
            value = cosine(angles[:, i * 128:(i + 1) * 128] + phase_ref[a, b:b + 1])
            natural[b, a] = value.astype(jnp.bfloat16)
            turned[a, b * 4:(b + 1) * 4] = value.T.astype(jnp.bfloat16).reshape(4, 2, 16, 128)

    batches = [(pl.ds(0, 1), None), (pl.ds(1, 2), pl.ds(2, 2)), (pl.ds(3, 4), pl.ds(4, 4))]
    shares = []
    for n, (slots, chunks) in enumerate(batches):
        for i, (dz, dk) in enumerate(mates):
            z2, k2 = (z + dz) % 4, (k + dk) % 2
            theirs = pl.ds(z2 // 2, 1) if chunks is None else chunks
            group = (me - (z2 * 2 + k2) + 8) % 8
            shares.append(remote(
                turned.at[z2 % 2 * 2 + k2, theirs], left_ref.at[slots, :, x, y, group],
                e_send.at[n], e_recv.at[n], device(x, y, z2, k2)))
    own_right = pltpu.make_async_copy(natural.at[slab], right_ref.at[me], own_sem)
    mate = device(x, y, z, k + 1)
    rights = []
    for i, dz in enumerate(hops):
        target = device(x, y, z + dz, k)
        rights.append(remote(natural.at[(z + dz) % 4 // 2], right_ref.at[me], r_sem.at[0], r_sem.at[1], target))
    rights.append(remote(natural.at[slab], right_ref.at[me], r_sem.at[0], r_sem.at[2], mate))
    handed = []
    for i, dz in enumerate(hops):
        at = right_ref.at[(z + dz) % 4 * 2 + k]
        handed.append(remote(at, at, r_sem.at[3], r_sem.at[2], mate))

    for b in range(2):
        features(b, row // 2)
    left_ref[0, :, x, y, 0] = turned[row, slab]
    left_ref[1:7, :, x, y, 0] = turned[row, 2:8]

    px, mx, py, my = along_x[0], along_x[1], along_y[0], along_y[1]
    xp, xm, yp, ym = (x + 1) % 4, (x + 3) % 4, (y + 1) % 4, (y + 3) % 4

    def copies(slot, number):
        if slot is OWN:
            def part(h, at_x, at_y, half=None):
                slots = {None: pl.ds(0, 7), 0: pl.ds(0, 4), 1: pl.ds(4, 3)}[half]
                return left_ref.at[slots, h, at_x, at_y, 0]
        else:
            def part(h, at_x, at_y, half=None):
                groups = {None: pl.ds(1, 7), 0: pl.ds(1, 3), 1: pl.ds(4, 4)}[half]
                return left_ref.at[slot, h, at_x, at_y, groups]
        low, high = pl.ds(0, 2), pl.ds(2, 2)
        if number == 0:
            pairs = [(part(0, x, y), px), (part(0, x, y), mx), (part(1, x, y), py), (part(1, x, y), my)]
        elif number == 1:
            pairs = [(part(0, xm, y, 0), px), (part(0, xp, y, 1), mx), (part(1, x, ym, 0), py), (part(1, x, yp, 1), my)]
        elif number == 2:
            pairs = [(part(0, low, y), py), (part(0, high, y), my), (part(1, x, low), px), (part(1, x, high), mx)]
        elif number == 3:
            pairs = [(part(0, low, ym), py), (part(0, high, yp), my), (part(1, xm, low), px), (part(1, xp, high), mx)]
        else:
            pairs = [(part(0, high, y), py), (part(0, low, y), my), (part(1, x, high), px), (part(1, x, low), mx)]
        place = order(slot)
        send, recv = g_send.at[place % 2, number], g_recv.at[place, number]
        return [remote(ref, ref, send, recv, target) for ref, target in pairs]

    def order(slot):
        return 0 if slot is OWN else slot + 1

    def whole(number):
        blocks = left_ref.at[0, 0, :, :, pl.ds(1, 7)]
        return (blocks.at[0], blocks.at[0, 0:2], blocks.at[0:2], blocks.at[0:2], blocks.at[0:2])[number]

    def received(slot, number):
        taken(whole(number), g_recv.at[order(slot), number])

    def crossing(h, half):
        return remote(
            left_ref.at[0, h, :, :, pl.ds(half * 4, 4)], left_ref.at[7, h, :, :, pl.ds(4 - half * 4, 4)],
            x_sem.at[0], x_sem.at[1], device(x, y, z + 2, k))

    crossings = [crossing(h, half) for h in range(2) for half in range(2)]

    def exchanged(n):
        return left_ref.at[batches[n][0], :, x, y, pl.ds(1, 7)]

    def wait_shares(n):
        taken(exchanged(n), e_recv.at[n])

    def multiply(slot, number, count=2):
        b, quarter = number // 4, number % 4
        rows = chunk_rows(left_ref, slot)
        for out_ref, at, factor in ((instant_ref, 0, 1.0 / 1024), (lagged_ref, 512, scale[0]))[:count]:
            total = jnp.dot(rows, columns[:, at:at + 512], preferred_element_type=jnp.float32) * factor
            for c in range(16):
                for a in range(4):
                    part = total[c * 32:(c + 1) * 32, a * 128:(a + 1) * 128]
                    out_ref[b, c, quarter, pl.ds(a, 32, stride=4), :] = part

    def advance(slot, number):
        if number < 5:
            if number > 0:
                received(slot, number - 1)
            elif slot is not OWN:
                for n, at in enumerate((0, 1, 3)):
                    pl.when(slot == at)(functools.partial(wait_shares, n))
            for sent in (2, 4) if number == 2 else (number,):
                if slot is not OWN:
                    @pl.when(slot >= 1)
                    def _():
                        taken(whole(sent), g_send.at[order(slot) % 2, sent])

                for copy in copies(slot, sent):
                    copy.start()
            return
        for sent in (4, 3):
            received(slot, sent)
        if slot is not OWN:
            @pl.when(slot == 0)
            def _():
                for copy in crossings:
                    copy.start()

    def rounds(numbers, step, _):
        for number in numbers:
            slot = step - min(number, 4) - 1
            pl.when(slot == -1)(functools.partial(advance, OWN, number))
            pl.when(jnp.logical_and(slot >= 0, slot < 7))(functools.partial(advance, slot, number))
        return 0

    early = functools.partial(rounds, (2, 1, 0, 3))
    steady = functools.partial(rounds, (0, 1, 2, 3, 5))

    def job(n, _):
        slot = n + jnp.where(n == 5, 2, 0) - jnp.where(n == 6, 1, 0)

        @pl.when(n == 5)
        def _():
            taken(left_ref.at[7], x_sem.at[1])

        @pl.when(n < 6)
        def _():
            multiply(slot, jnp.where(slot == 7, 1 - slab, jnp.where(slot == 0, slab, slot + 1)))

        @pl.when(n == 6)
        def _():
            multiply(5, 6, 1)

        return 0

    def later(step, _):
        steady(step, 0)
        begin = step - 6 + jnp.where(step >= 8, 1, 0)
        end = step - 5 + jnp.where(step >= 7, 1, 0) + jnp.where(step == 10, 1, 0)
        lax.fori_loop(begin, end, job, 0)
        return 0

    advance(OWN, 0)
    for b in range(2):
        features(b, 1 - row // 2)
    for copy in shares[:14]:
        copy.start()
    lax.fori_loop(1, 2, early, 0)
    for copy in shares[14:] + rights:
        copy.start()
    own_right.start()
    lax.fori_loop(2, 4, early, 0)
    lax.fori_loop(4, 5, steady, 0)
    taken(right_ref.at[0:3], r_sem.at[1])
    for copy in handed:
        copy.start()
    lax.fori_loop(5, 6, steady, 0)
    own_right.wait()
    taken(right_ref.at[0:4], r_sem.at[2])
    right_columns(right_ref, segment_ref, columns, scale, me)
    taken(d_all.at[:, 0, 0:3], d_sem.at[1])
    taken(d_all.at[:, 0:3], d_sem.at[0])
    for n in range(3):
        taken(exchanged(n), e_send.at[n])
    taken(right_ref.at[0:4], r_sem.at[0])
    taken(right_ref.at[0:3], r_sem.at[3])
    lax.fori_loop(6, 11, later, 0)
    taken(left_ref.at[7], x_sem.at[0])
    lax.fori_loop(11, 12, steady, 0)
    for place in range(2):
        for number in range(5):
            taken(whole(number), g_send.at[place, number])


def chunk_rows(left_ref, slot):
    return jnp.concatenate(
        [
            jnp.concatenate([left_ref[slot, h, x, y, g] for g in range(8)], 1)
            for x in range(4) for y in range(4) for h in range(2)
        ],
        0,
    )


def paired_before(segment_ref):
    ids = jnp.broadcast_to(segment_ref[...], (8, 1024))
    frame = lax.broadcasted_iota(jnp.int32, (8, 1024), 1)
    return jnp.where((pltpu.roll(ids, LAG, 1) == ids) & (frame >= LAG), 1.0, 0.0)[0:1]


def right_columns(right_ref, segment_ref, columns, scale, me):
    paired = paired_before(segment_ref)
    scale[0] = 1.0 / jnp.sum(paired)

    def wide(g):
        return jnp.concatenate([right_ref[g, a] for a in range(4)], 1)

    for n in range(8):
        at = pl.ds(pl.multiple_of((n - me + 8) % 8 * 128, 128), 128)
        columns[at, 0:512] = wide(n)
        g = min(n, 6)
        here = lax.broadcasted_iota(jnp.int32, (128, 256), 0) + n * 128
        there = lax.broadcasted_iota(jnp.int32, (128, 256), 1) + g * 128
        take = jnp.where(there == here + LAG, paired[:, g * 128:g * 128 + 256], 0.0).astype(jnp.bfloat16)
        both = jnp.concatenate([wide(g), wide(g + 1)], 0)
        columns[at, 512:1024] = jnp.dot(take, both, preferred_element_type=jnp.float32).astype(jnp.bfloat16)


OWN = "own"
TILES = (2, 16, 4, 128, 128)


def gather(distances, projection, phases, segment_ids):
    bf16, f32 = jnp.bfloat16, jnp.float32
    dma = pltpu.SemaphoreType.DMA
    anywhere = pl.BlockSpec(memory_space=pl.ANY)
    vmem = pl.BlockSpec(memory_space=pltpu.VMEM)
    return pl.pallas_call(
        gather_kernel,
        out_shape=(
            pltpu.VMEM(TILES, f32),
            pltpu.VMEM(TILES, f32),
            pltpu.VMEM((8, 2, 4, 4, 8, 16, 128), bf16),
            pltpu.VMEM((1024, 1024), bf16),
        ),
        in_specs=[anywhere] * 4,
        out_specs=(vmem,) * 4,
        scratch_shapes=[
            pltpu.VMEM((4, 2, 128), f32),
            pltpu.VMEM((1, 1024), jnp.int32),
            pltpu.VMEM((32768, 128), bf16),
            pltpu.VMEM((4, 4096, 256), bf16),
            pltpu.VMEM((2, 4, 4, 8, 2048), bf16),
            pltpu.VMEM((128, 4096), bf16),
            pltpu.VMEM((2, 4, 128, 128), bf16),
            pltpu.VMEM((4, 8, 2, 16, 128), bf16),
            pltpu.VMEM((8, 4, 128, 128), bf16),
            pltpu.SMEM((1,), f32),
            dma((3,)),
            dma((4,)),
            dma((3,)),
            dma((2, 3)),
            dma((3,)),
            dma((3,)),
            dma((4,)),
            dma((2, 5)),
            dma((8, 5)),
            dma((2,)),
            dma,
        ],
        compiler_params=pltpu.CompilerParams(
            collective_id=0, has_side_effects=True, vmem_limit_bytes=36 * MIB
        ),
        name="gather_features",
    )(distances, projection, phases, segment_ids)


def finish_kernel(
    instant_tiles, lagged_tiles, left_ref, columns, segment_ref, instant_ref, lagged_ref, last, sem
):
    copies = []

    def move(source, target, n):
        copy = pltpu.make_async_copy(source, target, sem.at[n])
        copy.start()
        copies.append(copy)

    outs = ((instant_tiles, instant_ref), (lagged_tiles, lagged_ref))
    for i, (tiles, out_ref) in enumerate(outs):
        move(tiles.at[0], out_ref.at[0], i * 3)
        done = pl.ds(0, 3 - i)
        move(tiles.at[1, :, done], out_ref.at[1, :, done], i * 3 + 1)
    inverse = 1.0 / jnp.sum(paired_before(segment_ref))
    for n, (slot, i) in enumerate(((5, 1), (6, 0), (6, 1))):
        rows = chunk_rows(left_ref, slot)
        total = jnp.dot(rows, columns[:, i * 512:(i + 1) * 512], preferred_element_type=jnp.float32)
        total = total * (inverse if i else 1.0 / 1024)
        for c in range(16):
            for a in range(4):
                last[n, c, pl.ds(a, 32, stride=4), :] = total[c * 32:(c + 1) * 32, a * 128:(a + 1) * 128]
        move(last.at[n], outs[i][1].at[1, :, slot - 3], (2, 5, 6)[n])
    for copy in copies:
        copy.wait()


def finish(tiles, segment_ids):
    out = jax.ShapeDtypeStruct(TILES, jnp.float32)
    vmem = pl.BlockSpec(memory_space=pltpu.VMEM)
    anywhere = pl.BlockSpec(memory_space=pl.ANY)
    return pl.pallas_call(
        finish_kernel,
        out_shape=(out, out),
        in_specs=[vmem] * 5,
        out_specs=(anywhere, anywhere),
        scratch_shapes=[
            pltpu.VMEM((3, 16, 128, 128), jnp.float32),
            pltpu.SemaphoreType.DMA((7,)),
        ],
        compiler_params=pltpu.CompilerParams(vmem_limit_bytes=5 * MIB),
        name="covariances",
    )(*tiles, segment_ids)


def per_device(distances, projection, phases, segment_ids):
    segments = segment_ids.reshape(1, 1024)
    tiles = gather(distances, projection.reshape(32768, 128), phases, segments)
    tiles = [pltpu.with_memory_space_constraint(part, pltpu.VMEM) for part in tiles]
    instant, lagged = finish(tiles, segments)
    return instant.reshape(4096, 4, 1, 128), lagged.reshape(4096, 4, 1, 128)


def solution(mesh):
    placed = (
        P(("slab", "row", "col"), None),
        P(None, None, None, "col"),
        P(None, None, "col"),
        P(),
    )
    return jax.shard_map(
        per_device,
        mesh=mesh,
        in_specs=placed,
        out_specs=(P("row", None, "slab", "col"), P("row", None, "slab", "col")),
        check_vma=False,
    )
```

```python
import functools

import jax
import jax.numpy as jnp
from jax import lax
from jax.experimental import pallas as pl
from jax.experimental.pallas import tpu as pltpu
from jax.sharding import PartitionSpec as P

LAG = 50
MESH = pl.DeviceIdType.MESH
MIB = 1 << 20
PI_A, PI_B, PI_C = 3.140625, 0.0009670257568359375, 6.2771141529083252e-07
COS_POLY = (
    2.08767570e-09, -2.75573192e-07, 2.48015873e-05, -1.38888889e-03, 4.16666667e-02, -0.5, 1.0
)


def cosine(angle):
    k = jnp.floor(angle * (1.0 / 3.14159265358979) + 0.5)
    r = ((angle - k * PI_A) - k * PI_B) - k * PI_C
    odd = k - 2.0 * jnp.floor(k * 0.5)
    square = r * r
    value = jnp.full_like(square, COS_POLY[0])
    for term in COS_POLY[1:]:
        value = value * square + term
    return value * (1.0 - 2.0 * odd)


def positions():
    slab, row, col = lax.axis_index("slab"), lax.axis_index("row"), lax.axis_index("col")
    return col // 4, col % 4, slab * 2 + row // 2, row % 2


def device(x, y, z, k):
    x, y, z, k = x % 4, y % 4, z % 4, k % 2
    return (z // 2, (z % 2) * 2 + k, x * 4 + y)


def remote(src, dst, send, recv, target):
    return pltpu.make_async_remote_copy(
        src_ref=src, dst_ref=dst, send_sem=send, recv_sem=recv, device_id=target, device_id_type=MESH
    )


def taken(view, sem):
    pltpu.make_async_copy(view, view, sem).wait()


def gather_kernel(
    d_hbm, p_ref, phase_hbm, segment_hbm, instant_ref, lagged_ref, left_ref, columns,
    phase_ref, segment_ref, stage, planes, d_all, d_rows, natural, turned, right_ref, scale,
    in_sem, p_sem, d_sem, first_recv, e_send, e_recv, r_sem, g_send, g_recv, x_sem, own_sem,
):
    x, y, z, k = positions()
    me, slab, row = z * 2 + k, z // 2, z % 2 * 2 + k
    n_chunk = 4
    chunk = p_ref.shape[0] // n_chunk

    def p_copy(n):
        rows = pl.ds(n * chunk, chunk)
        return pltpu.make_async_copy(p_ref.at[rows], stage.at[rows], p_sem.at[n])

    phase_copy = pltpu.make_async_copy(phase_hbm, phase_ref, in_sem.at[0])
    segment_copy = pltpu.make_async_copy(segment_hbm, segment_ref, in_sem.at[1])
    own_depth = [d_hbm.at[:, pl.ds(h * 2048, 2048)] for h in range(2)]
    d_copies = [pltpu.make_async_copy(own_depth[h], d_all.at[h, x, y], in_sem.at[2]) for h in range(2)]
    for copy in d_copies + [phase_copy, segment_copy]:
        copy.start()
    for n in range(n_chunk):
        p_copy(n).start()

    hops = (1, 3, 2)
    along_x = [device(x + d, y, z, k) for d in hops]
    along_y = [device(x, y + d, z, k) for d in hops]
    mates = [(0, 1), (1, 0), (1, 1), (3, 0), (3, 1), (2, 0), (2, 1)]
    barrier = pltpu.get_barrier_semaphore()
    partners = along_x + along_y + [device(x, y, z + dz, k + dk) for dz, dk in mates]
    for partner in partners:
        pl.semaphore_signal(barrier, inc=1, device_id=partner, device_id_type=MESH)

    pl.semaphore_wait(barrier, len(partners))

    axes = (along_x, along_y)

    def send_block(h, source, block, line, recv):
        for i in range(3):
            remote(source, block, d_sem.at[0 if recv is None else 1], d_sem.at[2] if recv is None else recv(h, i), line[i]).start()

    for h in range(2):
        send_block(h, own_depth[h], d_all.at[h, x, y], axes[h], lambda h, i: first_recv.at[h, i])
    for h in range(2):
        send_block(h, own_depth[h], d_all.at[h, x, y], axes[1 - h], None)
    for i, hop in enumerate(hops):
        for h in range(2):
            from_x, from_y = ((x - hop) % 4, y) if h == 0 else (x, (y - hop) % 4)
            block = d_all.at[h, from_x, from_y]
            taken(block, first_recv.at[h, i])
            send_block(h, block, block, axes[1 - h], None)

    to = lax.broadcasted_iota(jnp.int32, (256, 256), 0)
    source = lax.broadcasted_iota(jnp.int32, (256, 256), 1)
    permute = jnp.where((to % 32) * 8 + to // 32 == source, 1.0, 0.0).astype(jnp.bfloat16)

    def sort_rows(n):
        rows = stage[pl.ds(pl.multiple_of(n * 1024, 1024), 1024), :]
        wide = jnp.concatenate([rows[q * 256:(q + 1) * 256] for q in range(4)], 1)
        out = jnp.dot(permute, wide, preferred_element_type=jnp.float32).astype(jnp.bfloat16)
        for a in range(4):
            for b in range(2):
                part = out[(a * 2 + b) * 32:(a * 2 + b + 1) * 32]
                lanes = slice(a % 2 * 128, a % 2 * 128 + 128)
                for q in range(4):
                    at = pl.ds(pl.multiple_of(n * 128 + q * 32, 32), 32)
                    planes[b * 2 + a // 2, at, lanes] = part[:, q * 128:(q + 1) * 128]

    def sort_chunk(n, _):
        p_copy(n).wait()
        for i in range(8):
            sort_rows(n * 8 + i)
        return 0

    lax.fori_loop(0, n_chunk, sort_chunk, 0)
    phase_copy.wait()
    segment_copy.wait()
    taken(d_all.at[:, 0:3], d_sem.at[2])
    taken(d_all.at[:, x, y], in_sem.at[2])
    for h in range(2):
        part = d_all[h].astype(jnp.float32).reshape(128, 2048)
        d_rows[:, h * 2048:(h + 1) * 2048] = part.astype(jnp.bfloat16)

    def features(b, p):
        angles = jnp.dot(d_rows[...], planes[b * 2 + p], preferred_element_type=jnp.float32)
        for i in range(2):
            a = p * 2 + i
            value = cosine(angles[:, i * 128:(i + 1) * 128] + phase_ref[a, b:b + 1])
            natural[b, a] = value.astype(jnp.bfloat16)
            turned[a, b * 4:(b + 1) * 4] = value.T.astype(jnp.bfloat16).reshape(4, 2, 16, 128)

    batches = [(pl.ds(0, 1), None), (pl.ds(1, 2), pl.ds(2, 2)), (pl.ds(3, 4), pl.ds(4, 4))]
    shares = []
    for n, (slots, chunks) in enumerate(batches):
        for i, (dz, dk) in enumerate(mates):
            z2, k2 = (z + dz) % 4, (k + dk) % 2
            theirs = pl.ds(z2 // 2, 1) if chunks is None else chunks
            group = (me - (z2 * 2 + k2) + 8) % 8
            shares.append(remote(
                turned.at[z2 % 2 * 2 + k2, theirs], left_ref.at[slots, :, x, y, group],
                e_send.at[n], e_recv.at[n], device(x, y, z2, k2)))
    own_right = pltpu.make_async_copy(natural.at[slab], right_ref.at[me], own_sem)
    mate = device(x, y, z, k + 1)
    rights = []
    for i, dz in enumerate(hops):
        target = device(x, y, z + dz, k)
        rights.append(remote(natural.at[(z + dz) % 4 // 2], right_ref.at[me], r_sem.at[0], r_sem.at[1], target))
    rights.append(remote(natural.at[slab], right_ref.at[me], r_sem.at[0], r_sem.at[2], mate))
    handed = []
    for i, dz in enumerate(hops):
        at = right_ref.at[(z + dz) % 4 * 2 + k]
        handed.append(remote(at, at, r_sem.at[3], r_sem.at[2], mate))

    for b in range(2):
        features(b, row // 2)
    left_ref[0, :, x, y, 0] = turned[row, slab]
    left_ref[1:7, :, x, y, 0] = turned[row, 2:8]

    px, mx, py, my = along_x[0], along_x[1], along_y[0], along_y[1]
    xp, xm, yp, ym = (x + 1) % 4, (x + 3) % 4, (y + 1) % 4, (y + 3) % 4

    def copies(slot, number):
        if slot is OWN:
            def part(h, at_x, at_y, half=None):
                slots = {None: pl.ds(0, 7), 0: pl.ds(0, 4), 1: pl.ds(4, 3)}[half]
                return left_ref.at[slots, h, at_x, at_y, 0]
        else:
            def part(h, at_x, at_y, half=None):
                groups = {None: pl.ds(1, 7), 0: pl.ds(1, 3), 1: pl.ds(4, 4)}[half]
                return left_ref.at[slot, h, at_x, at_y, groups]
        low, high = pl.ds(0, 2), pl.ds(2, 2)
        if number == 0:
            pairs = [(part(0, x, y), px), (part(0, x, y), mx), (part(1, x, y), py), (part(1, x, y), my)]
        elif number == 1:
            pairs = [(part(0, xm, y, 0), px), (part(0, xp, y, 1), mx), (part(1, x, ym, 0), py), (part(1, x, yp, 1), my)]
        elif number == 2:
            pairs = [(part(0, low, y), py), (part(0, high, y), my), (part(1, x, low), px), (part(1, x, high), mx)]
        elif number == 3:
            pairs = [(part(0, low, ym), py), (part(0, high, yp), my), (part(1, xm, low), px), (part(1, xp, high), mx)]
        else:
            pairs = [(part(0, high, y), py), (part(0, low, y), my), (part(1, x, high), px), (part(1, x, low), mx)]
        place = order(slot)
        send, recv = g_send.at[place % 2, number], g_recv.at[place, number]
        return [remote(ref, ref, send, recv, target) for ref, target in pairs]

    def order(slot):
        return 0 if slot is OWN else slot + 1

    def whole(number):
        blocks = left_ref.at[0, 0, :, :, pl.ds(1, 7)]
        return (blocks.at[0], blocks.at[0, 0:2], blocks.at[0:2], blocks.at[0:2], blocks.at[0:2])[number]

    def received(slot, number):
        taken(whole(number), g_recv.at[order(slot), number])

    def crossing(h, half):
        return remote(
            left_ref.at[0, h, :, :, pl.ds(half * 4, 4)], left_ref.at[7, h, :, :, pl.ds(4 - half * 4, 4)],
            x_sem.at[0], x_sem.at[1], device(x, y, z + 2, k))

    crossings = [crossing(h, half) for h in range(2) for half in range(2)]

    def exchanged(n):
        return left_ref.at[batches[n][0], :, x, y, pl.ds(1, 7)]

    def wait_shares(n):
        taken(exchanged(n), e_recv.at[n])

    def multiply(slot, number, count=2):
        b, quarter = number // 4, number % 4
        rows = chunk_rows(left_ref, slot)
        for out_ref, at, factor in ((instant_ref, 0, None), (lagged_ref, 512, scale[0]))[:count]:
            total = jnp.dot(rows, columns[:, at:at + 512], preferred_element_type=jnp.float32)
            total = total if factor is None else total * factor
            for c in range(16):
                for a in range(4):
                    part = total[c * 32:(c + 1) * 32, a * 128:(a + 1) * 128]
                    out_ref[b, c, quarter, pl.ds(a, 32, stride=4), :] = part

    def advance(slot, number):
        if number < 5:
            if number > 0:
                received(slot, number - 1)
            elif slot is not OWN:
                for n, at in enumerate((0, 1, 3)):
                    pl.when(slot == at)(functools.partial(wait_shares, n))
            for sent in (2, 4) if number == 2 else (number,):
                if slot is not OWN:
                    @pl.when(slot >= 1)
                    def _():
                        taken(whole(sent), g_send.at[order(slot) % 2, sent])

                for copy in copies(slot, sent):
                    copy.start()
            return
        for sent in (4, 3):
            received(slot, sent)
        if slot is not OWN:
            @pl.when(slot == 0)
            def _():
                for copy in crossings:
                    copy.start()

    def rounds(numbers, step, _):
        for number in numbers:
            slot = step - min(number, 4) - 1
            pl.when(slot == -1)(functools.partial(advance, OWN, number))
            pl.when(jnp.logical_and(slot >= 0, slot < 7))(functools.partial(advance, slot, number))
        return 0

    early = functools.partial(rounds, (2, 1, 0, 3))
    steady = functools.partial(rounds, (0, 1, 2, 3, 5))

    def job(n, _):
        slot = n + jnp.where(n == 5, 2, 0) - jnp.where(n == 6, 1, 0)

        @pl.when(n == 5)
        def _():
            taken(left_ref.at[7], x_sem.at[1])

        @pl.when(n < 6)
        def _():
            multiply(slot, jnp.where(slot == 7, 1 - slab, jnp.where(slot == 0, slab, slot + 1)))

        @pl.when(n == 6)
        def _():
            multiply(5, 6, 1)

        return 0

    def later(step, _):
        steady(step, 0)
        begin = step - 6 + jnp.where(step >= 8, 1, 0)
        end = step - 5 + jnp.where(step >= 7, 1, 0) + jnp.where(step == 10, 1, 0)
        lax.fori_loop(begin, end, job, 0)
        return 0

    advance(OWN, 0)
    for b in range(2):
        features(b, 1 - row // 2)
    for copy in shares[:14]:
        copy.start()
    lax.fori_loop(1, 2, early, 0)
    for copy in shares[14:] + rights:
        copy.start()
    own_right.start()
    lax.fori_loop(2, 4, early, 0)
    lax.fori_loop(4, 5, steady, 0)
    taken(right_ref.at[0:3], r_sem.at[1])
    for copy in handed:
        copy.start()
    lax.fori_loop(5, 6, steady, 0)
    own_right.wait()
    taken(right_ref.at[0:4], r_sem.at[2])
    right_columns(right_ref, segment_ref, columns, scale, me)
    taken(d_all.at[:, 0, 0:3], d_sem.at[1])
    taken(d_all.at[:, 0:3], d_sem.at[0])
    for n in range(3):
        taken(exchanged(n), e_send.at[n])
    taken(right_ref.at[0:4], r_sem.at[0])
    taken(right_ref.at[0:3], r_sem.at[3])
    lax.fori_loop(6, 11, later, 0)
    taken(left_ref.at[7], x_sem.at[0])
    lax.fori_loop(11, 12, steady, 0)
    for place in range(2):
        for number in range(5):
            taken(whole(number), g_send.at[place, number])


def chunk_rows(left_ref, slot):
    return jnp.concatenate(
        [
            jnp.concatenate([left_ref[slot, h, x, y, g] for g in range(8)], 1)
            for x in range(4) for y in range(4) for h in range(2)
        ],
        0,
    )


def paired_before(segment_ref):
    ids = jnp.broadcast_to(segment_ref[...], (8, 1024))
    frame = lax.broadcasted_iota(jnp.int32, (8, 1024), 1)
    return jnp.where((pltpu.roll(ids, LAG, 1) == ids) & (frame >= LAG), 1.0, 0.0)[0:1]


def right_columns(right_ref, segment_ref, columns, scale, me):
    paired = paired_before(segment_ref)
    scale[0] = 1.0 / jnp.sum(paired)

    def wide(g):
        return jnp.concatenate([right_ref[g, a] for a in range(4)], 1)

    for n in range(8):
        at = pl.ds(pl.multiple_of((n - me + 8) % 8 * 128, 128), 128)
        columns[at, 0:512] = (wide(n).astype(jnp.float32) * (1.0 / 1024)).astype(jnp.bfloat16)
        g = min(n, 6)
        here = lax.broadcasted_iota(jnp.int32, (128, 256), 0) + n * 128
        there = lax.broadcasted_iota(jnp.int32, (128, 256), 1) + g * 128
        take = jnp.where(there == here + LAG, paired[:, g * 128:g * 128 + 256], 0.0).astype(jnp.bfloat16)
        both = jnp.concatenate([wide(g), wide(g + 1)], 0)
        columns[at, 512:1024] = jnp.dot(take, both, preferred_element_type=jnp.float32).astype(jnp.bfloat16)


OWN = "own"
TILES = (2, 16, 4, 128, 128)


def gather(distances, projection, phases, segment_ids):
    bf16, f32 = jnp.bfloat16, jnp.float32
    dma = pltpu.SemaphoreType.DMA
    anywhere = pl.BlockSpec(memory_space=pl.ANY)
    vmem = pl.BlockSpec(memory_space=pltpu.VMEM)
    return pl.pallas_call(
        gather_kernel,
        out_shape=(
            pltpu.VMEM(TILES, f32),
            pltpu.VMEM(TILES, f32),
            pltpu.VMEM((8, 2, 4, 4, 8, 16, 128), bf16),
            pltpu.VMEM((1024, 1024), bf16),
        ),
        in_specs=[anywhere] * 4,
        out_specs=(vmem,) * 4,
        scratch_shapes=[
            pltpu.VMEM((4, 2, 128), f32),
            pltpu.VMEM((1, 1024), jnp.int32),
            pltpu.VMEM((32768, 128), bf16),
            pltpu.VMEM((4, 4096, 256), bf16),
            pltpu.VMEM((2, 4, 4, 8, 2048), bf16),
            pltpu.VMEM((128, 4096), bf16),
            pltpu.VMEM((2, 4, 128, 128), bf16),
            pltpu.VMEM((4, 8, 2, 16, 128), bf16),
            pltpu.VMEM((8, 4, 128, 128), bf16),
            pltpu.SMEM((1,), f32),
            dma((3,)),
            dma((4,)),
            dma((3,)),
            dma((2, 3)),
            dma((3,)),
            dma((3,)),
            dma((4,)),
            dma((2, 5)),
            dma((8, 5)),
            dma((2,)),
            dma,
        ],
        compiler_params=pltpu.CompilerParams(
            collective_id=0, has_side_effects=True, vmem_limit_bytes=36 * MIB
        ),
        name="gather_features",
    )(distances, projection, phases, segment_ids)


def finish_kernel(
    instant_tiles, lagged_tiles, left_ref, columns, segment_ref, instant_ref, lagged_ref, last, sem
):
    copies = []

    def move(source, target, n):
        copy = pltpu.make_async_copy(source, target, sem.at[n])
        copy.start()
        copies.append(copy)

    outs = ((instant_tiles, instant_ref), (lagged_tiles, lagged_ref))
    for i, (tiles, out_ref) in enumerate(outs):
        move(tiles.at[0], out_ref.at[0], i * 3)
        done = pl.ds(0, 3 - i)
        move(tiles.at[1, :, done], out_ref.at[1, :, done], i * 3 + 1)
    inverse = 1.0 / jnp.sum(paired_before(segment_ref))
    for n, (slot, i) in enumerate(((5, 1), (6, 0), (6, 1))):
        rows = chunk_rows(left_ref, slot)
        total = jnp.dot(rows, columns[:, i * 512:(i + 1) * 512], preferred_element_type=jnp.float32)
        total = total * inverse if i else total
        for c in range(16):
            for a in range(4):
                last[n, c, pl.ds(a, 32, stride=4), :] = total[c * 32:(c + 1) * 32, a * 128:(a + 1) * 128]
        move(last.at[n], outs[i][1].at[1, :, slot - 3], (2, 5, 6)[n])
    for copy in copies:
        copy.wait()


def finish(tiles, segment_ids):
    out = jax.ShapeDtypeStruct(TILES, jnp.float32)
    vmem = pl.BlockSpec(memory_space=pltpu.VMEM)
    anywhere = pl.BlockSpec(memory_space=pl.ANY)
    return pl.pallas_call(
        finish_kernel,
        out_shape=(out, out),
        in_specs=[vmem] * 5,
        out_specs=(anywhere, anywhere),
        scratch_shapes=[
            pltpu.VMEM((3, 16, 128, 128), jnp.float32),
            pltpu.SemaphoreType.DMA((7,)),
        ],
        compiler_params=pltpu.CompilerParams(vmem_limit_bytes=5 * MIB),
        name="covariances",
    )(*tiles, segment_ids)


def per_device(distances, projection, phases, segment_ids):
    segments = segment_ids.reshape(1, 1024)
    tiles = gather(distances, projection.reshape(32768, 128), phases, segments)
    tiles = [pltpu.with_memory_space_constraint(part, pltpu.VMEM) for part in tiles]
    instant, lagged = finish(tiles, segments)
    return instant.reshape(4096, 4, 1, 128), lagged.reshape(4096, 4, 1, 128)


def solution(mesh):
    placed = (
        P(("slab", "row", "col"), None),
        P(None, None, None, "col"),
        P(None, None, "col"),
        P(),
    )
    return jax.shard_map(
        per_device,
        mesh=mesh,
        in_specs=placed,
        out_specs=(P("row", None, "slab", "col"), P("row", None, "slab", "col")),
        check_vma=False,
    )
```
